512 devices in a mesh: grp: 32 (over y, x, core), row: 16 (over z).
Axes of the slice: x: 4, y: 4, z: 16, core: 2. Of those that a mesh axis runs over, the one named last changes fastest.
Arguments:
- embedded: bfloat16 [2048, 128, 768], P(('grp', 'row')), may hold values from -0.59765625 to 0.59765625
- cotangent: bfloat16 [2048, 128, 768], P(('grp', 'row')), may hold values from -6 to 6
- w_query: bfloat16 [768, 768], P('row'), may hold values from -1 to 1
- w_key: bfloat16 [768, 768], P('row'), may hold values from -1 to 1
- w_value: bfloat16 [768, 768], P('row'), may hold values from -0.21875 to 0.21875
- w_output: bfloat16 [768, 768], P('row'), may hold values from -0.21875 to 0.21875
- helpers: int32 [32], replicated, may hold values from 0 to 31, as said below
- helped_row_flag: int32 [2048], P(('grp', 'row')), may hold values from 0 to 1, as said below
- row_live: int32 [2048], P(('grp', 'row')), may hold values from 0 to 1, as said below
Outputs:
- layer_out: bfloat16 [2048, 128, 768], P(('grp', 'row'))
- grad_in: bfloat16 [2048, 128, 768], P(('grp', 'row'))
The draws below stay inside these ranges and needn't reach their ends.
Inputs may be any that keep to these rules, and one draw needn't show every extreme that they name: helpers names for each group the one MSA whose extra rows it may hold; it may name the group itself. `helped_row_flag`: the first slot of every device holds a row of its group's own MSA. `row_live`: the first slot of every device is live.
All inputs are finite; a program needn't handle non-finite values.
Results may differ from the reference program's by a relative error of at most 0.0085.
The reference program's roundings to bfloat16 on the way (of `normed`, `dattend`, `attend_b`, `dlogit` and `attended`) count: a program that leaves them out, or rounds other values in their place, can miss the bound.
Values may be sent and summed in bfloat16 or wider, within the bound.
A program may use at most 64 MiB of HBM per device.

```python
import math
import jax
import jax.numpy as jnp
from jax import lax

D = 768
HEADS = 12
L = 128
RDEV = 4
ROWS = 2048
N_GRP = 32


def helper_list(key):
    first = jax.random.randint(jax.random.fold_in(key, 11), (N_GRP,), 0, N_GRP)
    second = jax.random.randint(jax.random.fold_in(key, 12), (N_GRP,), 0, N_GRP)
    chosen = jnp.minimum(first, second)
    return chosen.at[0].set(N_GRP - 1).astype(jnp.int32)


def base_matrix(key):
    return jax.random.normal(jax.random.fold_in(key, 21), (D, D), jnp.float32)


def draw_helpers(key, part):
    listed = helper_list(key)
    return listed


def draw_helped_row_flag(key, part):
    key = jax.random.fold_in(key, 3)
    position = jnp.arange(ROWS, dtype=jnp.int32)
    slot_pos = position % RDEV
    toss_bits = jax.random.randint(key, (ROWS,), 0, 2)
    return jnp.where(slot_pos == 0, 0, toss_bits).astype(jnp.int32)


def draw_row_live(key, part):
    key = jax.random.fold_in(key, 5)
    position = jnp.arange(ROWS, dtype=jnp.int32)
    slot_pos = position % RDEV
    levels = jax.random.randint(key, (ROWS,), 0, 4)
    return jnp.where((slot_pos == 0) | (levels > 0), 1, 0).astype(jnp.int32)


def draw_w_query(key, part):
    shared = base_matrix(key)
    return (jnp.clip(shared, -6.0, 6.0) * D ** (-0.5)).astype(jnp.bfloat16)


def draw_w_key(key, part):
    key = jax.random.fold_in(key, 7)
    fresh = jax.random.normal(key, (D, D), jnp.float32)
    mixed = fresh
    return (jnp.clip(mixed, -6.0, 6.0) * D ** (-0.5)).astype(jnp.bfloat16)


def steps_of(key, shape, cuts, smallest, high):
    gain = 1.0
    for dim, blocks in cuts:
        draws = jax.random.uniform(jax.random.fold_in(jax.random.fold_in(key, 6), dim), (blocks,), jnp.float32, smallest / len(cuts), high / len(cuts))
        gain = gain * jnp.repeat(jnp.exp(draws), shape[dim] // blocks).reshape((-1,) + (1,) * (len(shape) - 1 - dim))
    return gain


def normal_values(stream_key, extent, width, bound, shards=(), kind=jnp.bfloat16):
    drawn = jax.random.normal(stream_key, extent, jnp.float32) * width
    if len(shards) > 0:
        drawn = steps_of(stream_key, extent, shards, -0.22, 0.18) * drawn
    return jnp.clip(drawn, min=-bound, max=bound).astype(kind)


def setup_inputs(seed: int = 0) -> dict:
    splits = jax.random.split(jax.random.key(seed), 10)
    embedded = normal_values(splits[0], (ROWS, L, D), 0.1, 0.59765625, ((0, 512),))
    cotangent = normal_values(splits[1], (ROWS, L, D), 1.0, 6.0, ((0, 512),))
    w_query = draw_w_query(jax.random.fold_in(splits[9], 71), 0)
    w_key = draw_w_key(jax.random.fold_in(splits[9], 71), 0)
    w_value = normal_values(splits[4], (D, D), D ** -0.5, 0.21875, ((0, 16),))
    w_output = normal_values(splits[5], (D, D), D ** -0.5, 0.21875, ((0, 16),))
    helpers = draw_helpers(jax.random.fold_in(splits[9], 71), 0)
    helped_row_flag = draw_helped_row_flag(jax.random.fold_in(splits[9], 71), 0)
    row_live = draw_row_live(jax.random.fold_in(splits[9], 71), 0)
    return {"embedded": embedded, "cotangent": cotangent, "w_query": w_query, "w_key": w_key, "w_value": w_value, "w_output": w_output, "helpers": helpers, "helped_row_flag": helped_row_flag, "row_live": row_live}


def layer_norm(rows_in):
    center = lax.optimization_barrier(jnp.mean(rows_in, axis=-1, keepdims=True))
    centred = rows_in - center
    spread = lax.optimization_barrier(jnp.mean(centred * centred, axis=-1, keepdims=True))
    return centred * lax.rsqrt(spread + 1e-05)

def project(left, weight):
    return jnp.dot(left, weight, preferred_element_type=jnp.float32)

def reference(embedded, cotangent, w_query, w_key, w_value, w_output, helpers, helped_row_flag, row_live):
    row_count = embedded.shape[0]
    length = embedded.shape[1]
    model_width = embedded.shape[2]
    head_size = model_width // HEADS
    head_shape = (row_count, length, HEADS, head_size)
    flat_in = embedded.astype(jnp.float32).reshape(row_count * length, model_width)
    normed_f, norm_back = jax.vjp(layer_norm, flat_in)
    normed = normed_f.astype(jnp.bfloat16)
    queries = project(normed, w_query).astype(jnp.bfloat16).reshape(head_shape)
    key_rows = project(normed, w_key).astype(jnp.bfloat16).reshape(head_shape)
    values = project(normed, w_value).astype(jnp.bfloat16).reshape(head_shape)
    flat_cot = cotangent.reshape(row_count * length, model_width)
    dattend = project(flat_cot, w_output.T).astype(jnp.bfloat16).reshape(head_shape)
    group_list = N_GRP
    group_lookup = (jnp.arange(row_count, dtype=jnp.int32) // (row_count // group_list)).astype(jnp.int32)
    alignment_rows = jnp.where(helped_row_flag == 1, helpers[group_lookup], group_lookup).astype(jnp.int32)
    owner_onehot = (alignment_rows[:, None] == jnp.arange(group_list, dtype=jnp.int32)[None, :]).astype(jnp.float32)
    live_rows = row_live.astype(jnp.float32)
    depths = lax.optimization_barrier(jnp.sum(owner_onehot * live_rows[:, None], axis=0))
    row_block_list = row_count // group_list

    def accumulate(running, block_index):
        row_shift = (block_index * row_block_list).astype(jnp.int32)
        q_block = lax.dynamic_slice_in_dim(queries, row_shift, row_block_list, 0).astype(jnp.float32)
        k_block = lax.dynamic_slice_in_dim(key_rows, row_shift, row_block_list, 0).astype(jnp.float32)
        v_block = lax.dynamic_slice_in_dim(values, row_shift, row_block_list, 0).astype(jnp.float32)
        d_block = lax.dynamic_slice_in_dim(dattend, row_shift, row_block_list, 0).astype(jnp.float32)
        hot_block = lax.dynamic_slice_in_dim(owner_onehot, row_shift, row_block_list, 0)
        live_block = lax.dynamic_slice_in_dim(live_rows, row_shift, row_block_list, 0)
        partial_s = jnp.einsum('rihd,rjhd->rhij', q_block * live_block[:, None, None, None], k_block)
        partial_g = jnp.einsum('rihd,rjhd->rhij', d_block, v_block)
        return ((running[0] + jnp.einsum('rm,rhij->mhij', hot_block, partial_s), running[1] + jnp.einsum('rm,rhij->mhij', hot_block, partial_g)), None)
    zeros = jnp.zeros((group_list, HEADS, length, length), jnp.float32)
    (scores, grads), _ = lax.scan(accumulate, (zeros, zeros), jnp.arange(group_list, dtype=jnp.int32))
    scaling = (1.0 / (math.sqrt(head_size) * jnp.sqrt(depths)))[:, None, None, None]
    attend = jax.nn.softmax(scores * scaling, axis=-1)
    dlogit = (attend * (grads - lax.optimization_barrier(jnp.sum(grads * attend, axis=-1, keepdims=True))) * scaling).astype(jnp.bfloat16)
    attend_b = attend.astype(jnp.bfloat16)

    def apply_rows(running, block_index):
        row_shift = (block_index * row_block_list).astype(jnp.int32)
        q_block = lax.dynamic_slice_in_dim(queries, row_shift, row_block_list, 0).astype(jnp.float32)
        k_block = lax.dynamic_slice_in_dim(key_rows, row_shift, row_block_list, 0).astype(jnp.float32)
        v_block = lax.dynamic_slice_in_dim(values, row_shift, row_block_list, 0).astype(jnp.float32)
        d_block = lax.dynamic_slice_in_dim(dattend, row_shift, row_block_list, 0).astype(jnp.float32)
        owned_block = lax.dynamic_slice_in_dim(alignment_rows, row_shift, row_block_list, 0).astype(jnp.int32)
        live_block = lax.dynamic_slice_in_dim(live_rows, row_shift, row_block_list, 0)[:, None, None, None]
        probs_block = attend_b[owned_block].astype(jnp.float32)
        dlog_block = dlogit[owned_block].astype(jnp.float32)
        attended = jnp.einsum('rhij,rjhd->rihd', probs_block, v_block).astype(jnp.bfloat16)
        dvalue = jnp.einsum('rhij,rihd->rjhd', probs_block, d_block).astype(jnp.bfloat16)
        dquery = (jnp.einsum('rhij,rjhd->rihd', dlog_block, k_block) * live_block).astype(jnp.bfloat16)
        dkey = (jnp.einsum('rhij,rihd->rjhd', dlog_block, q_block) * live_block).astype(jnp.bfloat16)
        return (running, (attended, dvalue, dquery, dkey))
    _, (attended, dvalue, dquery, dkey) = lax.scan(apply_rows, jnp.zeros((), jnp.float32), jnp.arange(group_list, dtype=jnp.int32))
    flat_shape = (row_count * length, model_width)
    attended = attended.reshape(flat_shape)
    layer_out = (flat_in + project(attended, w_output)).astype(jnp.bfloat16).reshape(embedded.shape)
    dnormed = project(dquery.reshape(flat_shape), w_query.T) + project(dkey.reshape(flat_shape), w_key.T) + project(dvalue.reshape(flat_shape), w_value.T)
    grad_in = (flat_cot.astype(jnp.float32) + norm_back(dnormed)[0]).astype(jnp.bfloat16).reshape(embedded.shape)
    return (layer_out, grad_in)
```

```python
import functools

import jax
import jax.numpy as jnp
from jax import lax
from jax.experimental import pallas as pl
from jax.experimental.pallas import tpu as pltpu
from jax.sharding import PartitionSpec as P

HEADS = 12
RDEV = 4
L = 128
D = 768
ZN = 16
SH = D // ZN
QC = D // 2
CH = HEADS * L // ZN
CS = 2 * CH + 8
CG = 2 * CH
PAIRS = HEADS // 2
MESH = pl.DeviceIdType.MESH
F32 = jnp.float32
BF16 = jnp.bfloat16
N_SEM = 256


def rem(a, n):
    return lax.rem(a + n, n)


def dot(a, b):
    return lax.dot_general(a, b, (((1,), (0,)), ((), ())), preferred_element_type=F32)


def dot_t(a, b):
    return lax.dot_general(a, b, (((1,), (1,)), ((), ())), preferred_element_type=F32)


def kernel(
    emb_in,
    cot_in,
    w_query,
    w_key,
    w_value,
    w_output,
    helpers,
    flag,
    live,
    out_ref,
    gin_ref,
    emb,
    cot,
    out,
    gin,
    weights,
    normed,
    queries,
    keys,
    values,
    dattend,
    s_part,
    g_part,
    s_chain,
    g_chain,
    s_plane,
    g_plane,
    s_cross,
    g_cross,
    s_tot,
    g_tot,
    attend,
    probs,
    dlog,
    attended,
    dquery,
    dkey,
    dvalue,
    dnormed,
    send_sems,
    recv_sems,
    own_sems,
):
    g = lax.axis_index("grp")
    z = lax.axis_index("row")
    core = lax.rem(g, 2)
    x = lax.rem(lax.div(g, 2), 4)
    y = lax.div(g, 8)
    sib = g + 1 - 2 * core

    def at(group, row):
        return {"grp": group, "row": row}

    def chip(dx, dy):
        return at((rem(y + dy, 4) * 4 + rem(x + dx, 4)) * 2 + core, z)

    hops = {d: at(g, rem(z + d, ZN)) for d in (5, -5, 1, -1, 2, -2, 3, -3)}
    up, down = hops[1], hops[-1]
    around = {
        (dx, dy): chip(dx, dy) for dx in (1, -1, 0) for dy in (1, -1, 0) if dx != 0 or dy != 0
    }
    other = at(sib, z)
    x_step = 1 - 2 * lax.rem(x + core, 2)
    y_step = 1 - 2 * lax.rem(y + core, 2)
    partners = (chip(x_step, 0), chip(0, y_step), chip(x_step, y_step))

    barrier = pltpu.get_barrier_semaphore()
    peers = [*hops.values(), *around.values(), other]
    for peer in peers:
        pl.semaphore_signal(barrier, inc=1, device_id=peer, device_id_type=MESH)

    started = []
    used = [0]

    def take(count):
        used[0] += count
        assert used[0] <= N_SEM
        return used[0] - count

    def send(src, dst, peer):
        index = take(1)
        copy = pltpu.make_async_remote_copy(
            src_ref=src,
            dst_ref=dst,
            send_sem=send_sems.at[index],
            recv_sem=recv_sems.at[index],
            device_id=peer,
            device_id_type=MESH,
        )
        copy.start()
        started.append(copy)
        return copy

    def wait(copies):
        for copy in copies:
            copy.wait_recv()

    own_rows = pl.ds(pl.multiple_of(z * SH, 16), SH)
    shards = [
        pltpu.make_async_copy(ref, weights.at[m, own_rows, :], own_sems.at[m])
        for m, ref in enumerate((w_query, w_key, w_value, w_output))
    ]
    get_emb = pltpu.make_async_copy(emb_in, emb, own_sems.at[4])
    get_cot = pltpu.make_async_copy(cot_in, cot, own_sems.at[5])
    for copy in (*shards, get_emb, get_cot):
        copy.start()
    for copy in shards:
        copy.wait()

    pl.semaphore_wait(barrier, len(peers))

    def w_piece(shard):
        return weights.at[
            2 * core + lax.rem(y, 2),
            pl.ds(pl.multiple_of(shard * SH, 16), SH),
            pl.ds(pl.multiple_of(lax.rem(x, 2) * QC, 128), QC),
        ]

    def w_rows(shard):
        return weights.at[pl.ds(2 * core, 2), pl.ds(pl.multiple_of(shard * SH, 16), SH), :]

    class Spread:
        def __init__(self, piece):
            self.piece = piece
            self.arriving = {}
            for hop in (5, -5, 1, -1, 2, -2):
                self.send(0, hop)

        def send(self, d, hop):
            ref = self.piece(d)
            self.arriving[d - hop] = send(ref, ref, hops[hop])

        def second(self):
            self.wait(5, -5)
            self.send(5, -3)
            for hop in (2, -2, 1, -1):
                for d in (5, -5):
                    self.send(d, hop)

        def wait(self, *which):
            for d in which:
                self.arriving[d].wait_recv()

    def weight_relay():
        in_a, in_s = {}, []

        def along(*dists):
            for d in dists:
                ref = w_piece(rem(z + d, ZN))
                in_a[d] = [send(ref, ref, peer) for peer in partners]

        def across(*dists):
            for d in dists:
                wait(in_a[d])
                ref = w_rows(rem(z + d, ZN))
                in_s.append(send(ref, ref, other))

        spread = Spread(lambda d: w_piece(rem(z + d, ZN)))
        yield
        for d in (1, -1, 2, -2):
            spread.wait(d)
            along(d)
        spread.second()
        along(5, -5)
        across(1, -1, 2, -2)
        across(5, -5)
        for d in (7, -7, 3, -3, 6, -6, 4, -4, 8):
            spread.wait(d)
            along(d)
        across(7, -7, 3, -3, 6, -6, 4, -4, 8)
        wait(in_s)

    def chain_sum(part, chain, total, counts):
        kind = chain.dtype
        if counts is None:
            streams = (pl.ds(0, CG),)
        else:
            streams = (pl.ds(0, CH), pl.ds(CH, CS - CH))

        def term(half, chunk):
            rows = pl.ds(pl.multiple_of(chunk * CH, 8), CH)
            if counts is None:
                return jnp.concatenate([part[0, rows, :], part[1, rows, :]], axis=0)
            if half == 1:
                return jnp.concatenate([part[1, rows, :], counts], axis=0)
            return part[0, rows, :]

        def chunk_of(way, s):
            return rem(z + 8 - s, ZN) if way == 0 else rem(z - 7 + s, ZN)

        last = (7, 6)
        flying = {}
        for s in range(9):
            for half in range(len(streams)):
                for way in range(2):
                    if s > last[way] + 1:
                        continue
                    slot = chain.at[way, s, streams[half]]
                    if s > 0:
                        flying[way, half].wait_recv()
                    if s > last[way]:
                        continue
                    here = term(half, chunk_of(way, s))
                    if s > 0:
                        here = slot[...].astype(F32) + here
                    slot[...] = here.astype(kind)
                    flying[way, half] = send(
                        slot, chain.at[way, s + 1, streams[half]], (up, down)[way]
                    )
            if s < 8:
                yield
        for half in range(len(streams)):
            total[streams[half], :] = (
                term(half, z)
                + chain[0, 8, streams[half], :].astype(F32)
                + chain[1, 7, streams[half], :].astype(F32)
            )

    def share_of(buf, d):
        return buf.at[:, pl.ds(pl.multiple_of(rem(z + d, ZN) * CH, 16), CH), :]

    def gather_ring(buf):
        for s in range(8):
            ref = share_of(buf, -s)
            copies = [send(ref, ref, up)]
            if s < 7:
                ref = share_of(buf, s)
                copies.append(send(ref, ref, down))
            yield
            wait(copies)

    target = helpers[g]
    sib_target = helpers[sib]

    def plane_sum(plane, cross, total, rows):
        lo, hi = pl.ds(0, CH), pl.ds(CH, rows - CH)
        plane[y, x] = total[...].astype(plane.dtype)

        def item(dx, dy, *part):
            return plane.at[(rem(y + dy, 4), rem(x + dx, 4), *part)]

        own = item(0, 0)
        first = {step: send(own, own, peer) for step, peer in around.items()}
        yield
        passed = []

        def relay(step, source, part):
            ref = item(*source, part)
            passed.append(send(ref, ref, around[step]))

        for step in first:
            first[step].wait_recv()
        for side in (0, 1, -1):
            relay((1, 0), (-1, side), lo)
            relay((0, 1), (side, -1), lo)
            relay((-1, 0), (1, side), hi)
            relay((0, -1), (side, 1), hi)
        relay((1, 1), (-1, -1), lo)
        relay((-1, 1), (1, -1), hi)
        yield
        wait(passed)

        def sums(me, its_target):
            def step(slot, carry):
                b, a = lax.div(slot, 4), lax.rem(slot, 4)
                group = slot * 2 + core
                w_home = jnp.where(helpers[group] == me, 1.0, 0.0)
                w_own = jnp.where(its_target == group, 1.0, 0.0)
                w_help = jnp.where(helpers[group] == its_target, 1.0, 0.0)
                item = plane.at[b, a]
                home, helped, *tally = carry
                first, second = item[0:CH, :].astype(F32), item[CH:CG, :].astype(F32)
                home = home + w_home * second
                helped = helped + w_own * first + w_help * second
                if rows == CS:
                    count = item[CG:CS, :]
                    tally = [
                        tally[0] + w_home * count,
                        tally[1] + w_own * count,
                        tally[2] + w_help * count,
                    ]
                return (home, helped, *tally)

            zero = jnp.zeros((CH, L), F32)
            none = jnp.zeros((8, L), F32)
            carry = (zero, zero) + ((none,) * 3 if rows == CS else ())
            home, helped, *tally = lax.fori_loop(0, 16, step, carry)
            if rows == CS:
                first = jnp.broadcast_to(tally[0][4:5, :], (8, L))
                second = jnp.broadcast_to(tally[1][0:1, :] + tally[2][4:5, :], (8, L))
                where = lax.broadcasted_iota(jnp.int32, (8, L), 0) < 4
                return home, helped, jnp.where(where, first, second)
            return home, helped, None

        home, helped, tally = sums(sib, sib_target)
        cross[0, 0:CH, :] = home
        cross[0, CH:CG, :] = helped
        if rows == CS:
            cross[0, CG:CS, :] = tally
        swap = send(cross.at[0], cross.at[1], other)
        home, helped, tally = sums(g, target)
        yield
        swap.wait_recv()
        total[0:CH, :] = total[0:CH, :] + home + cross[1, 0:CH, :]
        total[CH:CG, :] = helped + cross[1, CH:CG, :]
        if rows == CS:
            where = lax.broadcasted_iota(jnp.int32, (8, L), 0) < 4
            own = jnp.where(where, total[CG:CS, :], 0.0)
            total[CG:CS, :] = own + tally + cross[1, CG:CS, :]

    def step_on(task):
        return next(task, "done") != "done"

    def finish(task):
        for _ in task:
            pass

    is_home = [(flag[r] == 0) | (target == g) for r in range(RDEV)]
    alive = [live[r].astype(F32) for r in range(RDEV)]
    home_f = [jnp.where(h, 1.0, 0.0) for h in is_home]
    help_f = [1.0 - h for h in home_f]
    home_live = [h * a for h, a in zip(home_f, alive)]
    help_live = [h * a for h, a in zip(help_f, alive)]

    first_half = (lax.broadcasted_iota(jnp.int32, (1, L), 1) < L // 2).astype(F32)
    halves = (first_half, 1.0 - first_half)

    def norm(row):
        center = jnp.sum(row, axis=-1, keepdims=True) * (1.0 / D)
        centred = row - center
        spread = jnp.sum(centred * centred, axis=-1, keepdims=True) * (1.0 / D)
        rstd = lax.rsqrt(spread + 1e-05)
        return centred * rstd, rstd

    def normalise():
        get_emb.wait()

        @pl.loop(0, RDEV)
        def _(r):
            rows = pl.ds(pl.multiple_of(r * L, L), L)
            normed[rows, :] = norm(emb[r].astype(F32))[0].astype(BF16)

    def project(m, dst):
        @pl.loop(0, 3)
        def _(n):
            cols = pl.ds(pl.multiple_of(n * 256, 256), 256)
            dst[:, cols] = dot(normed[...], weights[m, :, cols]).astype(BF16)

    def project_back():
        get_cot.wait()

        @pl.loop(0, 3)
        def _(n):
            cols = pl.ds(pl.multiple_of(n * 256, 256), 256)
            dattend[:, cols] = dot_t(cot[...].reshape(RDEV * L, D), weights[3, cols, :]).astype(
                BF16
            )

    def pair_terms(left, right, home_w, help_w, part, centre):
        masks = [
            [(half * w).astype(BF16) for w in ws] for ws in (home_w, help_w) for half in halves
        ]

        @pl.loop(0, PAIRS)
        def _(p):
            cols = pl.ds(pl.multiple_of(p * L, L), L)
            lefts = jnp.concatenate(
                [left[r * L : (r + 1) * L, cols] for r in range(RDEV)], axis=1
            )
            rights = [right[r * L : (r + 1) * L, cols] for r in range(RDEV)]
            for v in range(4):
                masked = jnp.concatenate(
                    [rights[r] * masks[v][r] for r in range(RDEV)], axis=1
                )
                rows = pl.ds(pl.multiple_of(p * 2 * L + (v % 2) * L, L), L)
                sums = dot_t(lefts, masked)
                if centre:
                    sums = sums - jnp.sum(sums, axis=-1, keepdims=True) * (1.0 / L)
                part[v // 2, rows, :] = sums

    def split_heads(ref, r, cols):
        piece = ref[r * L : (r + 1) * L, cols]
        return jnp.concatenate([piece * half.astype(BF16) for half in halves], axis=0)

    def apply_pair(mix, first, first_out, second, second_out, scale, p):
        cols = pl.ds(pl.multiple_of(p * L, L), L)
        tiles = [
            [mix[e, pl.ds(pl.multiple_of((2 * p + h) * L, L), L), :] for h in range(2)]
            for e in range(2)
        ]
        straight = [jnp.concatenate(t, axis=1) for t in tiles]
        turned = [jnp.concatenate([t.T for t in ts], axis=1) for ts in tiles]
        for r in range(RDEV):
            rows = slice(r * L, (r + 1) * L)
            pick = jnp.where(is_home[r], straight[0], straight[1])
            one = dot(pick, split_heads(first, r, cols))
            pick = jnp.where(is_home[r], turned[0], turned[1])
            two = dot(pick, split_heads(second, r, cols))
            if scale is not None:
                one, two = one * scale[r], two * scale[r]
            first_out[rows, cols] = one.astype(BF16)
            second_out[rows, cols] = two.astype(BF16)

    relay = weight_relay()
    step_on(relay)
    normalise()
    finish(relay)

    project(0, queries)
    project(1, keys)
    pair_terms(queries, keys, home_live, help_live, s_part, False)

    where = lax.broadcasted_iota(jnp.int32, (8, L), 0) < 4
    home_count = home_live[0] + home_live[1] + home_live[2] + home_live[3]
    help_count = help_live[0] + help_live[1] + help_live[2] + help_live[3]
    counts = jnp.where(where, home_count, help_count)
    scalings = []
    own_share = pl.ds(pl.multiple_of(z * CH, 16), CH)

    def score_task():
        yield from chain_sum(s_part, s_chain, s_tot, counts)
        yield from plane_sum(s_plane, s_cross, s_tot, CS)
        for e in range(2):
            depth = s_tot[CG + 4 * e : CG + 4 * e + 1, :]
            scalings.append(1.0 / (8.0 * jnp.sqrt(depth)))
            logits = s_tot[e * CH : (e + 1) * CH, :] * scalings[e]
            top = jnp.exp(logits - jnp.max(logits, axis=-1, keepdims=True))
            share = top / jnp.sum(top, axis=-1, keepdims=True)
            attend[e] = share
            probs[e, own_share, :] = share.astype(BF16)
        yield from gather_ring(probs)

    def grad_task():
        yield from chain_sum(g_part, g_chain, g_tot, None)
        yield from plane_sum(g_plane, g_cross, g_tot, CG)
        for e in range(2):
            share = attend[e]
            grads = g_tot[e * CH : (e + 1) * CH, :]
            mean = jnp.sum(grads * share, axis=-1, keepdims=True)
            dlog[e, own_share, :] = (share * (grads - mean) * scalings[e]).astype(BF16)
        yield from gather_ring(dlog)

    scores, grads = score_task(), grad_task()
    step_on(scores)
    project(2, values)
    project_back()
    pair_terms(dattend, values, home_f, help_f, g_part, True)
    for _ in range(8):
        step_on(scores)
        step_on(grads)
    for task in (grads, scores, grads, scores, grads):
        step_on(task)
    for _ in range(8):
        step_on(scores)
        step_on(grads)
    finish(scores)

    @pl.loop(0, PAIRS)
    def _(p):
        apply_pair(probs, values, attended, dattend, dvalue, None, p)

    @pl.loop(0, 3)
    def _(n):
        cols = pl.ds(pl.multiple_of(n * 256, 256), 256)
        part = dot(attended[...], weights[3, :, cols])
        for r in range(RDEV):
            rows = slice(r * L, (r + 1) * L)
            out[r, :, cols] = (emb[r, :, cols].astype(F32) + part[rows, :]).astype(BF16)

    put_out = pltpu.make_async_copy(out, out_ref, own_sems.at[6])
    put_out.start()

    @pl.loop(0, 3)
    def _(n):
        cols = pl.ds(pl.multiple_of(n * 256, 256), 256)
        dnormed[:, cols] = dot_t(dvalue[...], weights[2, cols, :])

    finish(grads)

    @pl.loop(0, PAIRS)
    def _(p):
        apply_pair(dlog, keys, dquery, queries, dkey, alive, p)

    @pl.loop(0, 3)
    def _(n):
        cols = pl.ds(pl.multiple_of(n * 256, 256), 256)
        dnormed[:, cols] += dot_t(dquery[...], weights[0, cols, :]) + dot_t(
            dkey[...], weights[1, cols, :]
        )

    @pl.loop(0, RDEV)
    def _(r):
        rows = pl.ds(pl.multiple_of(r * L, L), L)
        unit, rstd = norm(emb[r].astype(F32))
        grad = dnormed[rows, :]
        mean = jnp.sum(grad, axis=-1, keepdims=True) * (1.0 / D)
        along = jnp.sum(grad * unit, axis=-1, keepdims=True) * (1.0 / D)
        back = rstd * (grad - mean - unit * along)
        gin[r] = (cot[r].astype(F32) + back).astype(BF16)
        pltpu.make_async_copy(gin.at[r], gin_ref.at[r], own_sems.at[7 + r]).start()

    put_out.wait()
    for r in range(RDEV):
        pltpu.make_async_copy(gin.at[r], gin_ref.at[r], own_sems.at[7 + r]).wait()

    for copy in started:
        copy.wait_send()


def per_device(*args):
    rows = RDEV * L
    hbm = pl.BlockSpec(memory_space=pl.ANY)
    smem = pl.BlockSpec(memory_space=pltpu.SMEM)
    shape = jax.ShapeDtypeStruct((RDEV, L, D), BF16)
    flat = pltpu.VMEM((rows, D), BF16)
    scratch = [
        pltpu.VMEM((RDEV, L, D), BF16),
        pltpu.VMEM((RDEV, L, D), BF16),
        pltpu.VMEM((RDEV, L, D), BF16),
        pltpu.VMEM((RDEV, L, D), BF16),
        pltpu.VMEM((4, D, D), BF16),
        flat,
        flat,
        flat,
        flat,
        flat,
        pltpu.VMEM((2, HEADS * L, L), F32),
        pltpu.VMEM((2, HEADS * L, L), F32),
        pltpu.VMEM((2, 9, CS, L), F32),
        pltpu.VMEM((2, 9, CG, L), BF16),
        pltpu.VMEM((4, 4, CS, L), F32),
        pltpu.VMEM((4, 4, CG, L), BF16),
        pltpu.VMEM((2, CS, L), F32),
        pltpu.VMEM((2, CG, L), F32),
        pltpu.VMEM((CS, L), F32),
        pltpu.VMEM((CG, L), F32),
        pltpu.VMEM((2, CH, L), F32),
        pltpu.VMEM((2, HEADS * L, L), BF16),
        pltpu.VMEM((2, HEADS * L, L), BF16),
        flat,
        flat,
        flat,
        flat,
        pltpu.VMEM((rows, D), F32),
        pltpu.SemaphoreType.DMA((N_SEM,)),
        pltpu.SemaphoreType.DMA((N_SEM,)),
        pltpu.SemaphoreType.DMA((11,)),
    ]
    return pl.pallas_call(
        kernel,
        out_shape=(shape, shape),
        in_specs=[hbm] * 6 + [smem] * 3,
        out_specs=(hbm, hbm),
        scratch_shapes=scratch,
        compiler_params=pltpu.CompilerParams(
            collective_id=0, has_side_effects=True, vmem_limit_bytes=56 * 1024 * 1024
        ),
    )(*args)


def solution(mesh):
    placed = (
        P(("grp", "row"), None, None),
        P(("grp", "row"), None, None),
        P("row", None),
        P("row", None),
        P("row", None),
        P("row", None),
        P(),
        P(("grp", "row")),
        P(("grp", "row")),
    )
    return jax.shard_map(
        per_device,
        mesh=mesh,
        in_specs=placed,
        out_specs=(P(("grp", "row"), None, None), P(("grp", "row"), None, None)),
        check_vma=False,
    )
```

```python
import functools

import jax
import jax.numpy as jnp
from jax import lax
from jax.experimental import pallas as pl
from jax.experimental.pallas import tpu as pltpu
from jax.sharding import PartitionSpec as P

HEADS = 12
RDEV = 4
L = 128
D = 768
ZN = 16
SH = D // ZN
QC = D // 2
CH = HEADS * L // ZN
PAIRS = HEADS // 2
MESH = pl.DeviceIdType.MESH
F32 = jnp.float32
BF16 = jnp.bfloat16
N_SEM = 400

PARTS = 2
PR = CH // PARTS
HALF = HEADS * L // PARTS
PP = PAIRS // PARTS
CHUNK = 3
S_STREAMS = 2
G_STREAMS = 1

W_TREE = {0: (3, 1, 2), 3: (3, 1, 2), 6: (1, 2)}
Z_TREE = {
    0: (3, -3, 1, -1),
    -3: (3, 1, -1),
    3: (-3, -1, 1),
    -6: (1, -1),
    6: (-1, 1),
    -7: (1,),
}
S_TREE = {0: (1, 2), **{k: (1,) for k in range(2, 8)}}
G_TREE = {k: (1,) for k in range(8)}
S_LEAD = 12
HOLD = 2
Z_HOPS = (1, -1, 2, -2, 3, -3)


class Plan:
    def __init__(self):
        self.now = 0.0
        self.free = {}
        self.tasks = []
        self.out = []
        self.marks = {}

    def book(self, kb, path):
        self.now += 0.1
        start, hops = self.now, 0
        for link, units, cores in path:
            hops += units
            span = kb / 600.0 if link == "core" else units * kb * cores / 100.0
            start = max(start, self.free.get(link, 0.0)) + span
            self.free[link] = start
        return start + 2.5 + 0.15 * (hops - 1)

    def spend(self, time):
        self.now += time

    def mark(self, name):
        self.marks[name] = round(self.now, 1)

    def spawn(self, rank, task):
        wanted = next(task, None)
        if wanted is not None:
            self.tasks.append([rank, task, wanted])

    def run(self, done):
        while not done():
            best = None
            for entry in self.tasks:
                due = max([copy.due for copy in entry[2]], default=0.0)
                key = (max(due, self.now), entry[0], due)
                if best is None or key < best[0]:
                    best = (key, entry)
            key, entry = best
            while self.out and self.now + 0.1 < key[0] and self.out[0].due < self.now:
                self.out.pop(0).copy.wait_send()
                self.now += 0.03
            self.now = max(self.now, key[0]) + 0.05 * len(entry[2])
            for copy in entry[2]:
                copy.wait()
            wanted = next(entry[1], None)
            if wanted is None:
                self.tasks.remove(entry)
            else:
                entry[2] = wanted


LAST_PLAN = []


class Flight:
    def __init__(self, copy, due):
        self.copy, self.due = copy, due

    def wait(self):
        self.copy.wait_recv()


def rem(a, n):
    return lax.rem(a + n, n)


def dot(a, b):
    return lax.dot_general(a, b, (((1,), (0,)), ((), ())), preferred_element_type=F32)


def dot_t(a, b):
    return lax.dot_general(a, b, (((1,), (1,)), ((), ())), preferred_element_type=F32)


def kernel(
    emb_in,
    cot_in,
    w_query,
    w_key,
    w_value,
    w_output,
    helpers,
    flag,
    live,
    out_ref,
    gin_ref,
    emb,
    cot,
    out,
    gin,
    weights,
    normed,
    queries,
    keys,
    values,
    dattend,
    s_part,
    g_part,
    s_chain,
    g_chain,
    s_plane,
    g_plane,
    s_cross,
    g_cross,
    s_tot,
    g_tot,
    attend,
    probs,
    dlog,
    attended,
    dquery,
    dkey,
    dvalue,
    dnormed,
    send_sems,
    recv_sems,
    own_sems,
):
    g = lax.axis_index("grp")
    z = lax.axis_index("row")
    core = lax.rem(g, 2)
    x = lax.rem(lax.div(g, 2), 4)
    y = lax.div(g, 8)
    sib = g + 1 - 2 * core
    way_of_core = 1 - 2 * core
    plan = Plan()
    LAST_PLAN[:] = [plan]

    def at(group, row):
        return {"grp": group, "row": row}

    def chip(dx, dy):
        return at((rem(y + dy, 4) * 4 + rem(x + dx, 4)) * 2 + core, z)

    hops = {d: at(g, rem(z + d, ZN)) for d in Z_HOPS}
    around = {
        (dx, dy): chip(dx, dy) for dx in (1, -1, 0) for dy in (1, -1, 0) if dx != 0 or dy != 0
    }
    other = at(sib, z)
    x_step = 1 - 2 * lax.rem(x + core, 2)
    y_step = 1 - 2 * lax.rem(y + core, 2)
    partners = (
        (chip(x_step, 0), (("wx", 1, 1),)),
        (chip(0, y_step), (("wy", 1, 1),)),
        (chip(x_step, y_step), (("wx", 1, 1), ("wy", 1, 1))),
    )

    barrier = pltpu.get_barrier_semaphore()
    peers = [*hops.values(), *around.values(), other]
    for peer in peers:
        pl.semaphore_signal(barrier, inc=1, device_id=peer, device_id_type=MESH)

    started = [0]
    steps = [0]

    def send(ref, dst, peer, kb, path):
        index = started[0]
        copy = pltpu.make_async_remote_copy(
            src_ref=ref,
            dst_ref=dst,
            send_sem=send_sems.at[index],
            recv_sem=recv_sems.at[index],
            device_id=peer,
            device_id_type=MESH,
        )
        copy.start()
        started[0] += 1
        flight = Flight(copy, plan.book(kb, path))
        plan.out.append(flight)
        return flight

    own_rows = pl.ds(pl.multiple_of(z * SH, 16), SH)
    shards = [
        pltpu.make_async_copy(ref, weights.at[m, own_rows, :], own_sems.at[m])
        for m, ref in enumerate((w_query, w_key, w_value, w_output))
    ]
    get_emb = pltpu.make_async_copy(emb_in, emb, own_sems.at[4])
    get_cot = pltpu.make_async_copy(cot_in, cot, own_sems.at[5])
    for copy in (*shards, get_emb, get_cot):
        copy.start()
    for copy in shards:
        copy.wait()

    pl.semaphore_wait(barrier, len(peers))

    arrived = [0, 0]

    def weight_set(m, rank):
        def rows(k):
            return pl.ds(pl.multiple_of(rem(z - way_of_core * k, ZN) * SH, 16), SH)

        def piece(k):
            columns = pl.ds(pl.multiple_of(lax.rem(x, 2) * QC, 128), QC)
            return weights.at[2 * m + lax.rem(y, 2), rows(k), columns]

        def forward(k):
            for hop in W_TREE.get(k, ()):
                ref = piece(k)
                peer = at(g, rem(z + way_of_core * hop, ZN))
                path = (("up", hop, 1),)
                flight = send(ref, ref, peer, 36.9, path)
                plan.free["down"] = plan.free.get("down", 0.0) + hop * 0.369
                plan.spawn(rank, arrive(k + hop, flight))

        def arrive(k, flight):
            yield [flight]
            forward(k)
            ref = piece(k)
            flights = [send(ref, ref, peer, 36.9, path) for peer, path in partners]
            yield flights
            if k < 8:
                ref = weights.at[pl.ds(2 * m, 2), rows(k), :]
                yield [send(ref, ref, other, 147.5, (("core", 1, 1),))]
            arrived[m] += 1

        forward(0)

    def chain_sum(part, chain, tree, p, counts, streams, rank, finished):
        kind = chain.dtype
        rows = chain.shape[3]
        edges = [0, rows] if streams == 1 else [0, PR, rows]
        left = [2 * streams]

        def term(lo, hi, chunk):
            span = pl.ds(pl.multiple_of(p * HALF + chunk * PR, 16), PR)
            pieces = []
            if lo < PR:
                pieces.append(part[0, span, :])
            if hi > PR:
                pieces.append(part[1, span, :])
            if hi > 2 * PR:
                pieces.append(counts)
            return jnp.concatenate(pieces, axis=0) if len(pieces) > 1 else pieces[0]

        nodes = (8, 7)
        below = [
            {
                k: [k + hop for hop in tree.get(k, ()) if k + hop <= nodes[way]]
                for k in range(nodes[way] + 1)
            }
            for way in range(2)
        ]

        def stream(way, lo, hi):
            span = pl.ds(lo, hi - lo)
            kb = (hi - lo) * L * (4 if kind == F32 else 2) / 1000.0
            sign = 1 - 2 * way
            above = {child: k for k, under in below[way].items() for child in under}
            flights = {}

            def pass_on(k):
                here = term(lo, hi, rem(z + sign * k, ZN))
                for child in below[way][k]:
                    here = here + chain[p, way, child - 1, span].astype(F32)
                slot = chain.at[p, way, 7 + k, span]
                slot[...] = here.astype(kind)
                plan.spend(0.04)
                hop = k - above[k]
                path = (("up" if way == 0 else "down", hop, 2),)
                landing = chain.at[p, way, k - 1, span]
                flights[k] = send(slot, landing, hops[sign * hop], kb, path)
                if all(child in flights for child in below[way][above[k]]):
                    plan.spawn(rank, node(above[k]))

            def node(k):
                yield [flights[child] for child in below[way][k]]
                if k > 0:
                    if kind == F32:
                        steps[0] += 1
                        lead()
                    pass_on(k)
                    return
                left[0] -= 1
                if left[0] == 0:
                    plan.spend(0.1)
                    total = term(0, rows, z)
                    for side in range(2):
                        for child in below[side][0]:
                            total = total + chain[p, side, child - 1].astype(F32)
                    finished(p, total)

            for k in range(nodes[way], 0, -1):
                if not below[way][k]:
                    pass_on(k)

        for lo, hi in zip(edges[:-1], edges[1:]):
            for way in range(2):
                stream(way, lo, hi)

    def spread(buf, tree, p, rank, finished):
        left = [15]

        def piece(d):
            start = pl.multiple_of(p * HALF + rem(z + d, ZN) * PR, 16)
            return buf.at[:, pl.ds(start, PR), :]

        def forward(d):
            for hop in tree.get(d, ()):
                ref = piece(d)
                path = (("up", hop, 2),) if hop > 0 else (("down", -hop, 2),)
                flight = send(ref, ref, hops[hop], PR * 0.512, path)
                plan.spawn(rank, arrive(d - hop, flight))

        def arrive(d, flight):
            yield [flight]
            forward(d)
            left[0] -= 1
            if left[0] == 0:
                finished(p)

        forward(0)

    target = helpers[g]
    sib_target = helpers[sib]
    top_half = lax.broadcasted_iota(jnp.int32, (8, L), 0) < 4

    def plane_sum(plane, cross, total, p, rank, finished):
        rows = 2 * PR + (8 if p == 0 and plane.dtype == F32 else 0)
        tallied = rows > 2 * PR
        kb = rows * L * (4 if plane.dtype == F32 else 2) / 1000.0
        lo, hi = pl.ds(0, PR), pl.ds(PR, rows - PR)
        passed = []
        left = [8]
        whole = pl.ds(0, rows)
        plane[p, y, x, whole] = total[p, whole].astype(plane.dtype)

        def path(dx, dy):
            steps = []
            if dx != 0:
                steps.append(("x+" if dx > 0 else "x-", 1, 2))
            if dy != 0:
                steps.append(("y+" if dy > 0 else "y-", 1, 2))
            return steps

        def item(dx, dy, *span):
            return plane.at[(p, rem(y + dy, 4), rem(x + dx, 4), *span)]

        def relay(step, source, span, share):
            ref = item(*source, span)
            passed.append(send(ref, ref, around[step], kb * share, path(*step)))

        def arrive(dx, dy, flight):
            yield [flight]
            source = (-dx, -dy)
            if dx != 0:
                relay((dx, 0), source, lo if dx > 0 else hi, 0.5)
            if dy != 0:
                relay((0, dy), source, lo if dy > 0 else hi, 0.5)
            if (dx, dy) == (1, 1):
                relay((1, 1), source, lo, 0.5)
            if (dx, dy) == (-1, 1):
                relay((-1, 1), source, hi, 0.5)
            left[0] -= 1
            if left[0] == 0:
                plan.spawn(rank, finish())
                if plane.dtype == F32:
                    state["sent"] += 1
                    release()

        def sums(me, its_target):
            def step(slot, carry):
                b, a = lax.div(slot, 4), lax.rem(slot, 4)
                group = slot * 2 + core
                w_home = jnp.where(helpers[group] == me, 1.0, 0.0)
                w_own = jnp.where(its_target == group, 1.0, 0.0)
                w_help = jnp.where(helpers[group] == its_target, 1.0, 0.0)
                share = plane.at[p, b, a]
                home, helped, *tally = carry
                first, second = share[0:PR, :].astype(F32), share[PR : 2 * PR, :].astype(F32)
                home = home + w_home * second
                helped = helped + w_own * first + w_help * second
                if tallied:
                    count = share[2 * PR : rows, :]
                    tally = [
                        tally[0] + w_home * count,
                        tally[1] + w_own * count,
                        tally[2] + w_help * count,
                    ]
                return (home, helped, *tally)

            zero = jnp.zeros((PR, L), F32)
            none = jnp.zeros((8, L), F32)
            carry = (zero, zero) + ((none,) * 3 if tallied else ())
            home, helped, *tally = lax.fori_loop(0, 16, step, carry)
            plan.spend(0.6 / PARTS)
            if tallied:
                first = jnp.broadcast_to(tally[0][4:5, :], (8, L))
                second = jnp.broadcast_to(tally[1][0:1, :] + tally[2][4:5, :], (8, L))
                return home, helped, jnp.where(top_half, first, second)
            return home, helped, None

        def finish():
            yield list(passed)
            home, helped, tally = sums(sib, sib_target)
            cross[p, 0, 0:PR, :] = home
            cross[p, 0, PR : 2 * PR, :] = helped
            if tallied:
                cross[p, 0, 2 * PR : rows, :] = tally
            swap = send(cross.at[p, 0, whole], cross.at[p, 1, whole], other, rows * 0.512, (("core", 1, 1),))
            home, helped, tally = sums(g, target)
            yield [swap]
            total[p, 0:PR, :] = total[p, 0:PR, :] + home + cross[p, 1, 0:PR, :]
            total[p, PR : 2 * PR, :] = helped + cross[p, 1, PR : 2 * PR, :]
            if tallied:
                own = jnp.where(top_half, total[p, 2 * PR : rows, :], 0.0)
                total[p, 2 * PR : rows, :] = own + tally + cross[p, 1, 2 * PR : rows, :]
            plan.spend(0.1)
            finished(p)

        for step, peer in around.items():
            own = item(0, 0, whole)
            plan.spawn(rank, arrive(*step, send(own, own, peer, kb, path(*step))))

    is_home = [(flag[r] == 0) | (target == g) for r in range(RDEV)]
    alive = [live[r].astype(F32) for r in range(RDEV)]
    home_f = [jnp.where(h, 1.0, 0.0) for h in is_home]
    help_f = [1.0 - h for h in home_f]
    home_live = [h * a for h, a in zip(home_f, alive)]
    help_live = [h * a for h, a in zip(help_f, alive)]
    home_count = home_live[0] + home_live[1] + home_live[2] + home_live[3]
    help_count = help_live[0] + help_live[1] + help_live[2] + help_live[3]
    counts = jnp.where(top_half, home_count, help_count)

    first_half = (lax.broadcasted_iota(jnp.int32, (1, L), 1) < L // 2).astype(F32)
    halves = (first_half, 1.0 - first_half)

    def norm(row):
        center = jnp.sum(row, axis=-1, keepdims=True) * (1.0 / D)
        centred = row - center
        spread_of = jnp.sum(centred * centred, axis=-1, keepdims=True) * (1.0 / D)
        rstd = lax.rsqrt(spread_of + 1e-05)
        return centred * rstd, rstd

    def normalise():
        plan.spend(1.2)

        @pl.loop(0, RDEV)
        def _(r):
            rows = pl.ds(pl.multiple_of(r * L, L), L)
            normed[rows, :] = norm(emb[r].astype(F32))[0].astype(BF16)

    def project(m, dst, p):
        plan.spend(0.5)

        @pl.loop(0, 2)
        def _(n):
            rows = pl.ds(pl.multiple_of(n * 256, 256), 256)
            cols = pl.ds(p * QC, QC)
            dst[rows, cols] = dot(normed[rows, :], weights[m, :, cols]).astype(BF16)

    def project_back():
        plan.spend(0.8)

        @pl.loop(0, 3)
        def _(n):
            cols = pl.ds(pl.multiple_of(n * 256, 256), 256)
            dattend[:, cols] = dot_t(cot[...].reshape(RDEV * L, D), weights[3, cols, :]).astype(
                BF16
            )

    def pair_terms(left, right, home_w, help_w, part, centre, first, last):
        plan.spend(0.1 * (last - first))
        masks = [
            [(half * w).astype(BF16) for w in ws] for ws in (home_w, help_w) for half in halves
        ]

        @pl.loop(first, last)
        def _(p):
            cols = pl.ds(pl.multiple_of(p * L, L), L)
            lefts = jnp.concatenate(
                [left[r * L : (r + 1) * L, cols] for r in range(RDEV)], axis=1
            )
            rights = [right[r * L : (r + 1) * L, cols] for r in range(RDEV)]
            for v in range(4):
                masked = jnp.concatenate(
                    [rights[r] * masks[v][r] for r in range(RDEV)], axis=1
                )
                rows = pl.ds(pl.multiple_of(p * 2 * L + (v % 2) * L, L), L)
                sums = dot_t(lefts, masked)
                if centre:
                    sums = sums - jnp.sum(sums, axis=-1, keepdims=True) * (1.0 / L)
                part[v // 2, rows, :] = sums

    def split_heads(ref, r, cols):
        piece = ref[r * L : (r + 1) * L, cols]
        return jnp.concatenate([piece * half.astype(BF16) for half in halves], axis=0)

    def apply_pair(mix, first, first_out, second, second_out, scale, p):
        cols = pl.ds(pl.multiple_of(p * L, L), L)
        tiles = [
            [mix[e, pl.ds(pl.multiple_of((2 * p + h) * L, L), L), :] for h in range(2)]
            for e in range(2)
        ]
        straight = [jnp.concatenate(t, axis=1) for t in tiles]
        turned = [jnp.concatenate([t.T for t in ts], axis=1) for ts in tiles]
        for r in range(RDEV):
            rows = slice(r * L, (r + 1) * L)
            pick = jnp.where(is_home[r], straight[0], straight[1])
            one = dot(pick, split_heads(first, r, cols))
            pick = jnp.where(is_home[r], turned[0], turned[1])
            two = dot(pick, split_heads(second, r, cols))
            if scale is not None:
                one, two = one * scale[r], two * scale[r]
            first_out[rows, cols] = one.astype(BF16)
            second_out[rows, cols] = two.astype(BF16)

    held = []
    state = {"sent": 0, "soft": set(), "grad": set(), "probs": 0, "dlog": 0, "applied": False}
    state.update(terms=False, led=False, late=list(range(PARTS)))
    scalings = []
    put_out = pltpu.make_async_copy(out, out_ref, own_sems.at[6])

    def share_rows(p):
        return pl.ds(pl.multiple_of(p * HALF + z * PR, 16), PR)

    def scores_summed(p, total):
        s_tot[p, 0 : total.shape[0], :] = total
        plan.mark(("scores summed", p))
        plane_sum(s_plane, s_cross, s_tot, p, 1, soften)

    def grads_summed(p, total):
        g_tot[p] = total
        plan.mark(("grads summed", p))
        held.append(p)
        release()

    def release():
        while held and state["sent"] >= HOLD:
            plane_sum(g_plane, g_cross, g_tot, held.pop(0), 2, grads_known)

    def soften(p):
        plan.spend(0.5 / PARTS)
        plan.mark(("softmax", p))
        for e in range(2):
            if p == 0:
                depth = s_tot[0, 2 * PR + 4 * e : 2 * PR + 4 * e + 1, :]
                scalings.append(1.0 / (8.0 * jnp.sqrt(depth)))
            logits = s_tot[p, e * PR : (e + 1) * PR, :] * scalings[e]
            top = jnp.exp(logits - jnp.max(logits, axis=-1, keepdims=True))
            share = top / jnp.sum(top, axis=-1, keepdims=True)
            attend[e, p * PR : (p + 1) * PR, :] = share
            probs[e, share_rows(p), :] = share.astype(BF16)
        state["soft"].add(p)
        spread(probs, Z_TREE, p, 3, probs_here)
        differentiate(p)

    def grads_known(p):
        state["grad"].add(p)
        differentiate(p)

    def differentiate(p):
        if p not in state["soft"] or p not in state["grad"]:
            return
        plan.spend(0.4 / PARTS)
        plan.mark(("dlogit", p))
        for e in range(2):
            share = attend[e, p * PR : (p + 1) * PR, :]
            grads = g_tot[p, e * PR : (e + 1) * PR, :]
            mean = jnp.sum(grads * share, axis=-1, keepdims=True)
            dlog[e, share_rows(p), :] = (share * (grads - mean) * scalings[e]).astype(BF16)
        spread(dlog, Z_TREE, p, 2, dlog_here)

    def probs_here(p):
        plan.mark(("probs", p))
        plan.spawn(9, apply_probs(p))

    def dlog_here(p):
        state["dlog"] += 1
        plan.mark(("dlog", p))
        if state["dlog"] < PARTS:
            state["late"].remove(p)
            plan.spawn(8, apply_dlog(p))

    def in_chunks(p, work):
        for first in range(p * PP, p * PP + PP, CHUNK):
            plan.spend(0.5 * CHUNK)

            @pl.loop(first, first + CHUNK)
            def _(pair):
                work(pair)

            yield []

    def apply_dlog(p):
        yield []
        yield from in_chunks(
            p, lambda pair: apply_pair(dlog, keys, dquery, queries, dkey, alive, pair)
        )

    def apply_probs(p):
        yield []
        yield from in_chunks(
            p, lambda pair: apply_pair(probs, values, attended, dattend, dvalue, None, pair)
        )
        state["probs"] += 1
        if state["probs"] < PARTS:
            return
        plan.spend(0.8)

        @pl.loop(0, 3)
        def _(n):
            cols = pl.ds(pl.multiple_of(n * 256, 256), 256)
            part = dot(attended[...], weights[3, :, cols])
            for r in range(RDEV):
                rows = slice(r * L, (r + 1) * L)
                out[r, :, cols] = (emb[r, :, cols].astype(F32) + part[rows, :]).astype(BF16)

        put_out.start()
        yield []
        plan.spend(0.8)

        @pl.loop(0, 3)
        def _(n):
            cols = pl.ds(pl.multiple_of(n * 256, 256), 256)
            dnormed[:, cols] = dot_t(dvalue[...], weights[2, cols, :])

        state["applied"] = True

    def grad_terms():
        yield []
        get_cot.wait()
        for p in range(PARTS):
            project(2, values, p)
            yield []
        project_back()
        yield []
        for p in range(PARTS):
            pair_terms(
                dattend, values, home_f, help_f, g_part, True, p * PP, p * PP + PP
            )
            yield []
        state["terms"] = True
        lead()

    def lead():
        if state["terms"] and steps[0] >= S_LEAD and not state["led"]:
            state["led"] = True
            for p in range(PARTS):
                chain_sum(g_part, g_chain, G_TREE, p, None, G_STREAMS, 2, grads_summed)

    plan.spend(3.0)
    weight_set(0, 0)
    weight_set(1, 4)
    get_emb.wait()
    normalise()
    plan.run(lambda: arrived[0] == 8)
    plan.mark("weights 0")
    for p in range(PARTS):
        project(0, queries, p)
        project(1, keys, p)
        pair_terms(queries, keys, home_live, help_live, s_part, False, p * PP, p * PP + PP)
        chain = s_chain.at[:, :, :, 0 : 2 * PR + (8 if p == 0 else 0)]
        chain_sum(s_part, chain, S_TREE, p, counts, S_STREAMS, 1, scores_summed)
    plan.run(lambda: arrived[1] == 8)
    plan.mark("weights 1")
    plan.spawn(9, grad_terms())
    plan.run(lambda: state["dlog"] == PARTS and not plan.tasks)
    plan.mark("all here")
    plan.spend(1.5 * len(state["late"]) + 1.6 + 1.5 + 1.0)

    for p in state["late"]:

        @pl.loop(p * PP, p * PP + PP)
        def _(pair):
            apply_pair(dlog, keys, dquery, queries, dkey, alive, pair)

    @pl.loop(0, 3)
    def _(n):
        cols = pl.ds(pl.multiple_of(n * 256, 256), 256)
        dnormed[:, cols] += dot_t(dquery[...], weights[0, cols, :]) + dot_t(
            dkey[...], weights[1, cols, :]
        )

    @pl.loop(0, RDEV)
    def _(r):
        rows = pl.ds(pl.multiple_of(r * L, L), L)
        unit, rstd = norm(emb[r].astype(F32))
        grad = dnormed[rows, :]
        mean = jnp.sum(grad, axis=-1, keepdims=True) * (1.0 / D)
        along = jnp.sum(grad * unit, axis=-1, keepdims=True) * (1.0 / D)
        back = rstd * (grad - mean - unit * along)
        gin[r] = (cot[r].astype(F32) + back).astype(BF16)
        pltpu.make_async_copy(gin.at[r], gin_ref.at[r], own_sems.at[7 + r]).start()

    for flight in plan.out:
        flight.copy.wait_send()
    put_out.wait()
    for r in range(RDEV):
        pltpu.make_async_copy(gin.at[r], gin_ref.at[r], own_sems.at[7 + r]).wait()


def per_device(*args):
    rows = RDEV * L
    hbm = pl.BlockSpec(memory_space=pl.ANY)
    smem = pl.BlockSpec(memory_space=pltpu.SMEM)
    shape = jax.ShapeDtypeStruct((RDEV, L, D), BF16)
    flat = pltpu.VMEM((rows, D), BF16)
    block = pltpu.VMEM((RDEV, L, D), BF16)
    s_rows, g_rows = 2 * PR + 8, 2 * PR
    scratch = [
        block,
        block,
        block,
        block,
        pltpu.VMEM((4, D, D), BF16),
        flat,
        flat,
        flat,
        flat,
        flat,
        pltpu.VMEM((2, HEADS * L, L), F32),
        pltpu.VMEM((2, HEADS * L, L), F32),
        pltpu.VMEM((PARTS, 2, 16, s_rows, L), F32),
        pltpu.VMEM((PARTS, 2, 16, g_rows, L), BF16),
        pltpu.VMEM((PARTS, 4, 4, s_rows, L), F32),
        pltpu.VMEM((PARTS, 4, 4, g_rows, L), BF16),
        pltpu.VMEM((PARTS, 2, s_rows, L), F32),
        pltpu.VMEM((PARTS, 2, g_rows, L), F32),
        pltpu.VMEM((PARTS, s_rows, L), F32),
        pltpu.VMEM((PARTS, g_rows, L), F32),
        pltpu.VMEM((2, CH, L), F32),
        pltpu.VMEM((2, HEADS * L, L), BF16),
        pltpu.VMEM((2, HEADS * L, L), BF16),
        flat,
        flat,
        flat,
        flat,
        pltpu.VMEM((rows, D), F32),
        pltpu.SemaphoreType.DMA((N_SEM,)),
        pltpu.SemaphoreType.DMA((N_SEM,)),
        pltpu.SemaphoreType.DMA((11,)),
    ]
    return pl.pallas_call(
        kernel,
        out_shape=(shape, shape),
        in_specs=[hbm] * 6 + [smem] * 3,
        out_specs=(hbm, hbm),
        scratch_shapes=scratch,
        compiler_params=pltpu.CompilerParams(
            collective_id=0, has_side_effects=True, vmem_limit_bytes=56 * 1024 * 1024
        ),
    )(*args)


def solution(mesh):
    placed = (
        P(("grp", "row"), None, None),
        P(("grp", "row"), None, None),
        P("row", None),
        P("row", None),
        P("row", None),
        P("row", None),
        P(),
        P(("grp", "row")),
        P(("grp", "row")),
    )
    return jax.shard_map(
        per_device,
        mesh=mesh,
        in_specs=placed,
        out_specs=(P(("grp", "row"), None, None), P(("grp", "row"), None, None)),
        check_vma=False,
    )
```

```python
import functools

import jax
import jax.numpy as jnp
from jax import lax
from jax.experimental import pallas as pl
from jax.experimental.pallas import tpu as pltpu
from jax.sharding import PartitionSpec as P

HEADS = 12
RDEV = 4
L = 128
D = 768
ZN = 16
SH = D // ZN
QC = D // 2
CH = HEADS * L // ZN
PAIRS = HEADS // 2
MESH = pl.DeviceIdType.MESH
F32 = jnp.float32
BF16 = jnp.bfloat16
N_SEM = 400

PARTS = 2
PR = CH // PARTS
HALF = HEADS * L // PARTS
PP = PAIRS // PARTS
CHUNK = 3
S_STREAMS = 2
G_STREAMS = 1

W_TREE = {0: (3, 1, 2), 3: (3, 1, 2), 6: (1, 2)}
Z_TREE = {
    0: (3, -3, 1, -1),
    -3: (3, 1, -1),
    3: (-3, -1, 1),
    -6: (1, -1),
    6: (-1, 1),
    -7: (1,),
}
S_TREE = {0: (1, 2), **{k: (1,) for k in range(2, 8)}}
G_TREE = {k: (1,) for k in range(8)}
S_LEAD = 12
HOLD = 2
Z_HOPS = (1, -1, 2, -2, 3, -3)


START = 0.13
G_BLOCKS = ((0,), (1,))


class Plan:
    def __init__(self):
        self.now = 0.0
        self.free = {}
        self.tasks = []
        self.out = []
        self.marks = {}

    def book(self, kb, path):
        self.now += START
        start, hops = self.now, 0
        for link, units, cores in path:
            hops += units
            span = kb / 600.0 if link == "core" else units * kb * cores / 100.0
            start = max(start, self.free.get(link, 0.0)) + span
            self.free[link] = start
        return start + 2.5 + 0.15 * (hops - 1)

    def spend(self, time):
        self.now += time

    def mark(self, name):
        self.marks[name] = round(self.now, 1)

    def spawn(self, rank, task):
        wanted = next(task, None)
        if wanted is not None:
            self.tasks.append([rank, task, wanted])

    def run(self, done):
        while not done():
            best = None
            for entry in self.tasks:
                due = max([copy.due for copy in entry[2]], default=0.0)
                key = (max(due, self.now), entry[0], due)
                if best is None or key < best[0]:
                    best = (key, entry)
            key, entry = best
            while self.out and self.now + 0.1 < key[0] and self.out[0].due < self.now:
                self.out.pop(0).copy.wait_send()
                self.now += 0.03
            self.now = max(self.now, key[0]) + 0.05 * len(entry[2])
            for copy in entry[2]:
                copy.wait()
            wanted = next(entry[1], None)
            if wanted is None:
                self.tasks.remove(entry)
            else:
                entry[2] = wanted


LAST_PLAN = []


class Flight:
    def __init__(self, copy, due):
        self.copy, self.due = copy, due

    def wait(self):
        self.copy.wait_recv()


def rem(a, n):
    return lax.rem(a + n, n)


def dot(a, b):
    return lax.dot_general(a, b, (((1,), (0,)), ((), ())), preferred_element_type=F32)


def dot_t(a, b):
    return lax.dot_general(a, b, (((1,), (1,)), ((), ())), preferred_element_type=F32)


def norm(row):
    center = jnp.sum(row, axis=-1, keepdims=True) * (1.0 / D)
    centred = row - center
    spread_of = jnp.sum(centred * centred, axis=-1, keepdims=True) * (1.0 / D)
    rstd = lax.rsqrt(spread_of + 1e-05)
    return centred * rstd, rstd


def finish_rows(emb, cot, proj, grads, out, gin):
    row = emb[0].astype(F32)
    out[0] = (row + proj[...]).astype(BF16)
    unit, rstd = norm(row)
    grad = grads[...]
    mean = jnp.sum(grad, axis=-1, keepdims=True) * (1.0 / D)
    along = jnp.sum(grad * unit, axis=-1, keepdims=True) * (1.0 / D)
    gin[0] = (cot[0].astype(F32) + rstd * (grad - mean - unit * along)).astype(BF16)


def kernel(
    emb_in,
    cot_in,
    w_query,
    w_key,
    w_value,
    w_output,
    helpers,
    flag,
    live,
    proj_ref,
    grad_ref,
    emb,
    cot,
    proj,
    weights,
    normed,
    queries,
    keys,
    values,
    dattend,
    s_part,
    g_part,
    s_chain,
    g_chain,
    s_plane,
    g_plane,
    s_cross,
    g_cross,
    s_tot,
    g_tot,
    attend,
    probs,
    dlog,
    attended,
    dquery,
    dkey,
    dvalue,
    dnormed,
    send_sems,
    recv_sems,
    own_sems,
):
    g = lax.axis_index("grp")
    z = lax.axis_index("row")
    core = lax.rem(g, 2)
    x = lax.rem(lax.div(g, 2), 4)
    y = lax.div(g, 8)
    sib = g + 1 - 2 * core
    way_of_core = 1 - 2 * core
    plan = Plan()
    LAST_PLAN[:] = [plan]

    def at(group, row):
        return {"grp": group, "row": row}

    def chip(dx, dy):
        return at((rem(y + dy, 4) * 4 + rem(x + dx, 4)) * 2 + core, z)

    hops = {d: at(g, rem(z + d, ZN)) for d in Z_HOPS}
    around = {
        (dx, dy): chip(dx, dy) for dx in (1, -1, 0) for dy in (1, -1, 0) if dx != 0 or dy != 0
    }
    other = at(sib, z)
    x_step = 1 - 2 * lax.rem(x + core, 2)
    y_step = 1 - 2 * lax.rem(y + core, 2)
    partners = (
        (chip(x_step, 0), (("wx", 1, 1),)),
        (chip(0, y_step), (("wy", 1, 1),)),
        (chip(x_step, y_step), (("wx", 1, 1), ("wy", 1, 1))),
    )

    barrier = pltpu.get_barrier_semaphore()
    peers = [*hops.values(), *around.values(), other]
    for peer in peers:
        pl.semaphore_signal(barrier, inc=1, device_id=peer, device_id_type=MESH)

    started = [0]
    steps = [0]

    def send(ref, dst, peer, kb, path):
        index = started[0]
        copy = pltpu.make_async_remote_copy(
            src_ref=ref,
            dst_ref=dst,
            send_sem=send_sems.at[index],
            recv_sem=recv_sems.at[index],
            device_id=peer,
            device_id_type=MESH,
        )
        copy.start()
        started[0] += 1
        flight = Flight(copy, plan.book(kb, path))
        plan.out.append(flight)
        return flight

    own_rows = pl.ds(pl.multiple_of(z * SH, 16), SH)
    shards = [
        pltpu.make_async_copy(ref, weights.at[m, own_rows, :], own_sems.at[m])
        for m, ref in enumerate((w_query, w_key, w_value, w_output))
    ]
    get_emb = pltpu.make_async_copy(emb_in, emb, own_sems.at[4])
    get_cot = pltpu.make_async_copy(cot_in, cot, own_sems.at[5])
    for copy in (*shards, get_emb, get_cot):
        copy.start()
    for copy in shards:
        copy.wait()

    pl.semaphore_wait(barrier, len(peers))

    arrived = [0, 0]

    def weight_set(m, rank):
        def rows(k):
            return pl.ds(pl.multiple_of(rem(z - way_of_core * k, ZN) * SH, 16), SH)

        def piece(k):
            columns = pl.ds(pl.multiple_of(lax.rem(x, 2) * QC, 128), QC)
            return weights.at[2 * m + lax.rem(y, 2), rows(k), columns]

        def forward(k):
            for hop in W_TREE.get(k, ()):
                ref = piece(k)
                peer = at(g, rem(z + way_of_core * hop, ZN))
                path = (("up", hop, 1),)
                flight = send(ref, ref, peer, 36.9, path)
                plan.free["down"] = plan.free.get("down", 0.0) + hop * 0.369
                plan.spawn(rank, arrive(k + hop, flight))

        def arrive(k, flight):
            yield [flight]
            forward(k)
            ref = piece(k)
            yield [send(ref, ref, peer, 36.9, path) for peer, path in partners]
            if k < 8:
                ref = weights.at[pl.ds(2 * m, 2), rows(k), :]
                yield [send(ref, ref, other, 147.5, (("core", 1, 1),))]
            arrived[m] += 1

        forward(0)

    def chain_sum(part, chain, tree, p, blocks, counts, streams, rank, finished):
        kind = chain.dtype
        rows = chain.shape[3]
        edges = [0, rows] if streams == 1 else [0, PR, rows]
        left = [2 * streams]

        def term(lo, hi, chunk):
            pieces = []
            for i, block in enumerate(blocks):
                span = pl.ds(pl.multiple_of(block * HALF + chunk * PR, 16), PR)
                for half in range(2):
                    if lo <= (2 * i + half) * PR < hi:
                        pieces.append(part[half, span, :])
            if hi > 2 * len(blocks) * PR:
                pieces.append(counts)
            return jnp.concatenate(pieces, axis=0) if len(pieces) > 1 else pieces[0]

        nodes = (8, 7)
        below = [
            {
                k: [k + hop for hop in tree.get(k, ()) if k + hop <= nodes[way]]
                for k in range(nodes[way] + 1)
            }
            for way in range(2)
        ]

        def stream(way, lo, hi):
            span = pl.ds(lo, hi - lo)
            kb = (hi - lo) * L * (4 if kind == F32 else 2) / 1000.0
            sign = 1 - 2 * way
            above = {child: k for k, under in below[way].items() for child in under}
            flights = {}

            def pass_on(k):
                here = term(lo, hi, rem(z + sign * k, ZN))
                for child in below[way][k]:
                    here = here + chain[p, way, child - 1, span].astype(F32)
                slot = chain.at[p, way, 7 + k, span]
                slot[...] = here.astype(kind)
                plan.spend(0.04)
                hop = k - above[k]
                path = (("up" if way == 0 else "down", hop, 2),)
                landing = chain.at[p, way, k - 1, span]
                flights[k] = send(slot, landing, hops[sign * hop], kb, path)
                if all(child in flights for child in below[way][above[k]]):
                    plan.spawn(rank, node(above[k]))

            def node(k):
                yield [flights[child] for child in below[way][k]]
                if k > 0:
                    if kind == F32:
                        steps[0] += 1
                        lead()
                    pass_on(k)
                    return
                left[0] -= 1
                if left[0] == 0:
                    plan.spend(0.1)
                    total = term(0, rows, z)
                    for side in range(2):
                        for child in below[side][0]:
                            total = total + chain[p, side, child - 1].astype(F32)
                    finished(p, total)

            for k in range(nodes[way], 0, -1):
                if not below[way][k]:
                    pass_on(k)

        for lo, hi in zip(edges[:-1], edges[1:]):
            for way in range(2):
                stream(way, lo, hi)

    def spread(buf, tree, p, rank, finished):
        left = [15]

        def piece(d):
            start = pl.multiple_of(p * HALF + rem(z + d, ZN) * PR, 16)
            return buf.at[:, pl.ds(start, PR), :]

        def forward(d):
            for hop in tree.get(d, ()):
                ref = piece(d)
                path = (("up", hop, 2),) if hop > 0 else (("down", -hop, 2),)
                flight = send(ref, ref, hops[hop], PR * 0.512, path)
                plan.spawn(rank, arrive(d - hop, flight))

        def arrive(d, flight):
            yield [flight]
            forward(d)
            left[0] -= 1
            if left[0] == 0:
                finished(p)

        forward(0)

    target = helpers[g]
    sib_target = helpers[sib]
    top_half = lax.broadcasted_iota(jnp.int32, (8, L), 0) < 4

    def plane_sum(plane, cross, total, p, pairs, rank, finished):
        rows = 2 * PR * pairs + (8 if p == 0 and plane.dtype == F32 else 0)
        tallied = rows > 2 * PR * pairs
        kb = rows * L * (4 if plane.dtype == F32 else 2) / 1000.0
        passed = []
        left = [8]
        whole = pl.ds(0, rows)
        plane[p, y, x, whole] = total[p, whole].astype(plane.dtype)

        def path(dx, dy):
            steps = []
            if dx != 0:
                steps.append(("x+" if dx > 0 else "x-", 1, 2))
            if dy != 0:
                steps.append(("y+" if dy > 0 else "y-", 1, 2))
            return steps

        def item(dx, dy, *span):
            return plane.at[(p, rem(y + dy, 4), rem(x + dx, 4), *span)]

        passes = {
            (-1, 0): ((1, 0),),
            (-1, 1): ((1, 0), (0, -1)),
            (1, -1): ((-1, 0), (0, 1)),
            (0, -1): ((0, 1),),
            (1, 1): ((-1, -1),),
        }

        def arrive(dx, dy, flight):
            yield [flight]
            for step in passes.get((-dx, -dy), ()):
                ref = item(-dx, -dy, whole)
                passed.append(send(ref, ref, around[step], kb, path(*step)))
            left[0] -= 1
            if left[0] == 0:
                plan.spawn(rank, finish())
                if plane.dtype == F32:
                    state["sent"] += 1
                    release()

        def sums(me, its_target):
            def step(slot, carry):
                b, a = lax.div(slot, 4), lax.rem(slot, 4)
                group = slot * 2 + core
                w_home = jnp.where(helpers[group] == me, 1.0, 0.0)
                w_own = jnp.where(its_target == group, 1.0, 0.0)
                w_help = jnp.where(helpers[group] == its_target, 1.0, 0.0)
                share = plane.at[p, b, a]
                sums_of, tally = list(carry[: 2 * pairs]), carry[2 * pairs :]
                for i in range(0, 2 * pairs, 2):
                    first = share[i * PR : (i + 1) * PR, :].astype(F32)
                    second = share[(i + 1) * PR : (i + 2) * PR, :].astype(F32)
                    sums_of[i] = sums_of[i] + w_home * second
                    sums_of[i + 1] = sums_of[i + 1] + w_own * first + w_help * second
                if tallied:
                    count = share[2 * PR : rows, :]
                    tally = (
                        tally[0] + w_home * count,
                        tally[1] + w_own * count,
                        tally[2] + w_help * count,
                    )
                return (*sums_of, *tally)

            zero = jnp.zeros((PR, L), F32)
            none = jnp.zeros((8, L), F32)
            carry = (zero,) * (2 * pairs) + ((none,) * 3 if tallied else ())
            carry = lax.fori_loop(0, 16, step, carry)
            plan.spend(0.3 * pairs)
            sums_of, tally = carry[: 2 * pairs], carry[2 * pairs :]
            if tallied:
                first = jnp.broadcast_to(tally[0][4:5, :], (8, L))
                second = jnp.broadcast_to(tally[1][0:1, :] + tally[2][4:5, :], (8, L))
                return sums_of, jnp.where(top_half, first, second)
            return sums_of, None

        def finish():
            yield list(passed)
            sums_of, tally = sums(sib, sib_target)
            for i in range(2 * pairs):
                cross[p, 0, i * PR : (i + 1) * PR, :] = sums_of[i]
            if tallied:
                cross[p, 0, 2 * PR : rows, :] = tally
            swap = send(
                cross.at[p, 0, whole],
                cross.at[p, 1, whole],
                other,
                rows * 0.512,
                (("core", 1, 1),),
            )
            sums_of, tally = sums(g, target)
            yield [swap]
            for i in range(2 * pairs):
                span = slice(i * PR, (i + 1) * PR)
                here = sums_of[i] + cross[p, 1, span, :]
                total[p, span, :] = total[p, span, :] + here if i % 2 == 0 else here
            if tallied:
                own = jnp.where(top_half, total[p, 2 * PR : rows, :], 0.0)
                total[p, 2 * PR : rows, :] = own + tally + cross[p, 1, 2 * PR : rows, :]
            plan.spend(0.1)
            finished(p)

        for step, peer in around.items():
            own = item(0, 0, whole)
            plan.spawn(rank, arrive(*step, send(own, own, peer, kb, path(*step))))

    is_home = [(flag[r] == 0) | (target == g) for r in range(RDEV)]
    alive = [live[r].astype(F32) for r in range(RDEV)]
    home_f = [jnp.where(h, 1.0, 0.0) for h in is_home]
    help_f = [1.0 - h for h in home_f]
    home_live = [h * a for h, a in zip(home_f, alive)]
    help_live = [h * a for h, a in zip(help_f, alive)]
    home_count = home_live[0] + home_live[1] + home_live[2] + home_live[3]
    help_count = help_live[0] + help_live[1] + help_live[2] + help_live[3]
    counts = jnp.where(top_half, home_count, help_count)

    first_half = (lax.broadcasted_iota(jnp.int32, (1, L), 1) < L // 2).astype(F32)
    halves = (first_half, 1.0 - first_half)

    def normalise():
        plan.spend(1.2)

        @pl.loop(0, RDEV)
        def _(r):
            rows = pl.ds(pl.multiple_of(r * L, L), L)
            normed[rows, :] = norm(emb[r].astype(F32))[0].astype(BF16)

    def project(m, dst, p):
        plan.spend(0.5)

        @pl.loop(0, 2)
        def _(n):
            rows = pl.ds(pl.multiple_of(n * 256, 256), 256)
            cols = pl.ds(p * QC, QC)
            dst[rows, cols] = dot(normed[rows, :], weights[m, :, cols]).astype(BF16)

    def project_back():
        plan.spend(0.8)

        @pl.loop(0, 3)
        def _(n):
            cols = pl.ds(pl.multiple_of(n * 256, 256), 256)
            dattend[:, cols] = dot_t(cot[...].reshape(RDEV * L, D), weights[3, cols, :]).astype(
                BF16
            )

    def pair_terms(left, right, home_w, help_w, part, centre, first, last):
        plan.spend(0.1 * (last - first))
        masks = [
            [(half * w).astype(BF16) for w in ws] for ws in (home_w, help_w) for half in halves
        ]

        @pl.loop(first, last)
        def _(p):
            cols = pl.ds(pl.multiple_of(p * L, L), L)
            lefts = jnp.concatenate(
                [left[r * L : (r + 1) * L, cols] for r in range(RDEV)], axis=1
            )
            rights = [right[r * L : (r + 1) * L, cols] for r in range(RDEV)]
            for v in range(4):
                masked = jnp.concatenate(
                    [rights[r] * masks[v][r] for r in range(RDEV)], axis=1
                )
                rows = pl.ds(pl.multiple_of(p * 2 * L + (v % 2) * L, L), L)
                sums = dot_t(lefts, masked)
                if centre:
                    sums = sums - jnp.sum(sums, axis=-1, keepdims=True) * (1.0 / L)
                part[v // 2, rows, :] = sums

    def split_heads(ref, r, cols):
        piece = ref[r * L : (r + 1) * L, cols]
        return jnp.concatenate([piece * half.astype(BF16) for half in halves], axis=0)

    def apply_pair(mix, first, first_out, second, second_out, scale, p):
        cols = pl.ds(pl.multiple_of(p * L, L), L)
        tiles = [
            [mix[e, pl.ds(pl.multiple_of((2 * p + h) * L, L), L), :] for h in range(2)]
            for e in range(2)
        ]
        straight = [jnp.concatenate(t, axis=1) for t in tiles]
        turned = [jnp.concatenate([t.T for t in ts], axis=1) for ts in tiles]
        for r in range(RDEV):
            rows = slice(r * L, (r + 1) * L)
            pick = jnp.where(is_home[r], straight[0], straight[1])
            one = dot(pick, split_heads(first, r, cols))
            pick = jnp.where(is_home[r], turned[0], turned[1])
            two = dot(pick, split_heads(second, r, cols))
            if scale is not None:
                one, two = one * scale[r], two * scale[r]
            first_out[rows, cols] = one.astype(BF16)
            second_out[rows, cols] = two.astype(BF16)

    held = []
    state = {"sent": 0, "soft": set(), "grad": set(), "probs": 0, "dlog": 0, "applied": False}
    state.update(terms=False, led=False, late=list(range(PARTS)))
    scalings = []
    put_proj = pltpu.make_async_copy(proj, proj_ref, own_sems.at[6])

    def share_rows(p):
        return pl.ds(pl.multiple_of(p * HALF + z * PR, 16), PR)

    def scores_summed(p, total):
        s_tot[p, 0 : total.shape[0], :] = total
        plan.mark(("scores summed", p))
        plane_sum(s_plane, s_cross, s_tot, p, 1, 1, soften)

    def grads_summed(p, total):
        g_tot[p] = total
        plan.mark(("grads summed", p))
        held.append(p)
        release()

    def release():
        while held and state["sent"] >= HOLD:
            i = held.pop(0)
            plane_sum(g_plane, g_cross, g_tot, i, len(G_BLOCKS[i]), 2, grads_known)

    def soften(p):
        plan.spend(0.5 / PARTS)
        plan.mark(("softmax", p))
        for e in range(2):
            if p == 0:
                depth = s_tot[0, 2 * PR + 4 * e : 2 * PR + 4 * e + 1, :]
                scalings.append(1.0 / (8.0 * jnp.sqrt(depth)))
            logits = s_tot[p, e * PR : (e + 1) * PR, :] * scalings[e]
            top = jnp.exp(logits - jnp.max(logits, axis=-1, keepdims=True))
            share = top / jnp.sum(top, axis=-1, keepdims=True)
            attend[e, p * PR : (p + 1) * PR, :] = share
            probs[e, share_rows(p), :] = share.astype(BF16)
        state["soft"].add(p)
        spread(probs, Z_TREE, p, 3, probs_here)
        differentiate(p)

    def grads_known(i):
        for p in G_BLOCKS[i]:
            state["grad"].add(p)
            differentiate(p)

    def grads_of(p, e):
        for i, blocks in enumerate(G_BLOCKS):
            if p in blocks:
                start = (2 * blocks.index(p) + e) * PR
                return g_tot[i, start : start + PR, :]

    def differentiate(p):
        if p not in state["soft"] or p not in state["grad"]:
            return
        plan.spend(0.4 / PARTS)
        plan.mark(("dlogit", p))
        for e in range(2):
            share = attend[e, p * PR : (p + 1) * PR, :]
            grads = grads_of(p, e)
            mean = jnp.sum(grads * share, axis=-1, keepdims=True)
            dlog[e, share_rows(p), :] = (share * (grads - mean) * scalings[e]).astype(BF16)
        spread(dlog, Z_TREE, p, 2, dlog_here)

    def probs_here(p):
        plan.mark(("probs", p))
        plan.spawn(9, apply_probs(p))

    def dlog_here(p):
        state["dlog"] += 1
        plan.mark(("dlog", p))
        if state["dlog"] < PARTS:
            state["late"].remove(p)
            plan.spawn(8, apply_dlog(p))

    def in_chunks(p, work):
        for first in range(p * PP, p * PP + PP, CHUNK):
            plan.spend(0.5 * CHUNK)

            @pl.loop(first, first + CHUNK)
            def _(pair):
                work(pair)

            yield []

    def apply_dlog(p):
        yield []
        yield from in_chunks(
            p, lambda pair: apply_pair(dlog, keys, dquery, queries, dkey, alive, pair)
        )

    def apply_probs(p):
        yield []
        yield from in_chunks(
            p, lambda pair: apply_pair(probs, values, attended, dattend, dvalue, None, pair)
        )
        state["probs"] += 1
        if state["probs"] < PARTS:
            return
        plan.spend(0.8)

        @pl.loop(0, 3)
        def _(n):
            cols = pl.ds(pl.multiple_of(n * 256, 256), 256)
            proj[:, cols] = dot(attended[...], weights[3, :, cols])

        put_proj.start()
        yield []
        plan.spend(0.8)

        @pl.loop(0, 3)
        def _(n):
            cols = pl.ds(pl.multiple_of(n * 256, 256), 256)
            dnormed[:, cols] = dot_t(dvalue[...], weights[2, cols, :])

        state["applied"] = True

    def grad_terms():
        yield []
        get_cot.wait()
        for p in range(PARTS):
            project(2, values, p)
            yield []
        project_back()
        yield []
        for p in range(PARTS):
            pair_terms(
                dattend, values, home_f, help_f, g_part, True, p * PP, p * PP + PP
            )
            yield []
        state["terms"] = True
        lead()

    def lead():
        if state["terms"] and steps[0] >= S_LEAD and not state["led"]:
            state["led"] = True
            for i, blocks in enumerate(G_BLOCKS):
                chain_sum(
                    g_part, g_chain, G_TREE, i, blocks, None, G_STREAMS, 2, grads_summed
                )

    def put_grad(n):
        cols = pl.ds(pl.multiple_of(n * 256, 256), 256)
        return pltpu.make_async_copy(dnormed.at[:, cols], grad_ref.at[:, cols], own_sems.at[7 + n])

    plan.spend(3.0)
    weight_set(0, 0)
    weight_set(1, 4)
    get_emb.wait()
    normalise()
    plan.run(lambda: arrived[0] == 8)
    plan.mark("weights 0")
    for p in range(PARTS):
        project(0, queries, p)
        project(1, keys, p)
        pair_terms(queries, keys, home_live, help_live, s_part, False, p * PP, p * PP + PP)
        chain = s_chain.at[:, :, :, 0 : 2 * PR + (8 if p == 0 else 0)]
        chain_sum(s_part, chain, S_TREE, p, (p,), counts, S_STREAMS, 1, scores_summed)
    plan.run(lambda: arrived[1] == 8)
    plan.mark("weights 1")
    plan.spawn(9, grad_terms())
    plan.run(lambda: state["dlog"] == PARTS and not plan.tasks)
    plan.mark("all here")
    plan.spend(1.5 * len(state["late"]) + 1.6 + 1.5 + 1.0)

    for p in state["late"]:

        @pl.loop(p * PP, p * PP + PP)
        def _(pair):
            apply_pair(dlog, keys, dquery, queries, dkey, alive, pair)

    @pl.loop(0, 3)
    def _(n):
        cols = pl.ds(pl.multiple_of(n * 256, 256), 256)
        dnormed[:, cols] += dot_t(dquery[...], weights[0, cols, :]) + dot_t(
            dkey[...], weights[1, cols, :]
        )
        put_grad(n).start()

    for flight in plan.out:
        flight.copy.wait_send()
    put_proj.wait()
    for n in range(3):
        put_grad(n).wait()


def per_device(*args):
    rows = RDEV * L
    hbm = pl.BlockSpec(memory_space=pl.ANY)
    smem = pl.BlockSpec(memory_space=pltpu.SMEM)
    wide = jax.ShapeDtypeStruct((rows, D), F32)
    flat = pltpu.VMEM((rows, D), BF16)
    block = pltpu.VMEM((RDEV, L, D), BF16)
    s_rows, g_rows = 2 * PR + 8, 2 * PR * len(G_BLOCKS[0])
    scratch = [
        block,
        block,
        pltpu.VMEM((rows, D), F32),
        pltpu.VMEM((4, D, D), BF16),
        flat,
        flat,
        flat,
        flat,
        flat,
        pltpu.VMEM((2, HEADS * L, L), F32),
        pltpu.VMEM((2, HEADS * L, L), F32),
        pltpu.VMEM((PARTS, 2, 16, s_rows, L), F32),
        pltpu.VMEM((len(G_BLOCKS), 2, 16, g_rows, L), BF16),
        pltpu.VMEM((PARTS, 4, 4, s_rows, L), F32),
        pltpu.VMEM((len(G_BLOCKS), 4, 4, g_rows, L), BF16),
        pltpu.VMEM((PARTS, 2, s_rows, L), F32),
        pltpu.VMEM((len(G_BLOCKS), 2, g_rows, L), F32),
        pltpu.VMEM((PARTS, s_rows, L), F32),
        pltpu.VMEM((len(G_BLOCKS), g_rows, L), F32),
        pltpu.VMEM((2, CH, L), F32),
        pltpu.VMEM((2, HEADS * L, L), BF16),
        pltpu.VMEM((2, HEADS * L, L), BF16),
        flat,
        flat,
        flat,
        flat,
        pltpu.VMEM((rows, D), F32),
        pltpu.SemaphoreType.DMA((N_SEM,)),
        pltpu.SemaphoreType.DMA((N_SEM,)),
        pltpu.SemaphoreType.DMA((10,)),
    ]
    proj, grads = pl.pallas_call(
        kernel,
        out_shape=(wide, wide),
        in_specs=[hbm] * 6 + [smem] * 3,
        out_specs=(hbm, hbm),
        scratch_shapes=scratch,
        compiler_params=pltpu.CompilerParams(
            collective_id=0, has_side_effects=True, vmem_limit_bytes=48 * 1024 * 1024
        ),
    )(*args)
    shape = jax.ShapeDtypeStruct((RDEV, L, D), BF16)
    row = pl.BlockSpec((1, L, D), lambda r: (r, 0, 0))
    flat_row = pl.BlockSpec((L, D), lambda r: (r, 0))
    return pl.pallas_call(
        finish_rows,
        grid=(RDEV,),
        out_shape=(shape, shape),
        in_specs=[row, row, flat_row, flat_row],
        out_specs=(row, row),
        compiler_params=pltpu.CompilerParams(vmem_limit_bytes=16 * 1024 * 1024),
    )(args[0], args[1], proj, grads)


def solution(mesh):
    placed = (
        P(("grp", "row"), None, None),
        P(("grp", "row"), None, None),
        P("row", None),
        P("row", None),
        P("row", None),
        P("row", None),
        P(),
        P(("grp", "row")),
        P(("grp", "row")),
    )
    return jax.shard_map(
        per_device,
        mesh=mesh,
        in_specs=placed,
        out_specs=(P(("grp", "row"), None, None), P(("grp", "row"), None, None)),
        check_vma=False,
    )
```

```python
import functools

import jax
import jax.numpy as jnp
from jax import lax
from jax.experimental import pallas as pl
from jax.experimental.pallas import tpu as pltpu
from jax.sharding import PartitionSpec as P

HEADS = 12
RDEV = 4
L = 128
D = 768
ZN = 16
SH = D // ZN
QC = D // 2
CH = HEADS * L // ZN
PAIRS = HEADS // 2
MESH = pl.DeviceIdType.MESH
F32 = jnp.float32
BF16 = jnp.bfloat16
N_SEM = 400

PARTS = 2
PR = CH // PARTS
HALF = HEADS * L // PARTS
PP = PAIRS // PARTS
CHUNK = 3
S_STREAMS = 2
G_STREAMS = 1

W_TREE = {0: (3, 1, 2), 3: (3, 1, 2), 6: (1, 2)}
Z_TREE = {
    0: (3, -3, 1, -1),
    -3: (3, 1, -1),
    3: (-3, -1, 1),
    -6: (1, -1),
    6: (-1, 1),
    -7: (1,),
}
S_TREE = {0: (1, 2), **{k: (1,) for k in range(2, 8)}}
G_TREE = {k: (1,) for k in range(8)}
S_LEAD = 12
HOLD = 2
Z_HOPS = (1, -1, 2, -2, 3, -3)


START = 0.13
G_BLOCKS = ((0,), (1,))


class Plan:
    def __init__(self):
        self.now = 0.0
        self.free = {}
        self.tasks = []
        self.out = []
        self.marks = {}

    def book(self, kb, path):
        self.now += START
        start, hops = self.now, 0
        for link, units, cores in path:
            hops += units
            span = kb / 600.0 if link == "core" else units * kb * cores / 100.0
            start = max(start, self.free.get(link, 0.0)) + span
            self.free[link] = start
        return start + 2.5 + 0.15 * (hops - 1)

    def spend(self, time):
        self.now += time

    def mark(self, name):
        self.marks[name] = round(self.now, 1)

    def spawn(self, rank, task):
        wanted = next(task, None)
        if wanted is not None:
            self.tasks.append([rank, task, wanted])

    def run(self, done):
        while not done():
            best = None
            for entry in self.tasks:
                due = max([copy.due for copy in entry[2]], default=0.0)
                key = (max(due, self.now), entry[0], due)
                if best is None or key < best[0]:
                    best = (key, entry)
            key, entry = best
            while self.out and self.now + 0.1 < key[0] and self.out[0].due < self.now:
                self.out.pop(0).copy.wait_send()
                self.now += 0.03
            self.now = max(self.now, key[0]) + 0.05 * len(entry[2])
            for copy in entry[2]:
                copy.wait()
            wanted = next(entry[1], None)
            if wanted is None:
                self.tasks.remove(entry)
            else:
                entry[2] = wanted


LAST_PLAN = []


class Flight:
    def __init__(self, copy, due):
        self.copy, self.due = copy, due

    def wait(self):
        self.copy.wait_recv()


def rem(a, n):
    return lax.rem(a + n, n)


def dot(a, b):
    return lax.dot_general(a, b, (((1,), (0,)), ((), ())), preferred_element_type=F32)


def dot_t(a, b):
    return lax.dot_general(a, b, (((1,), (1,)), ((), ())), preferred_element_type=F32)


def norm(row):
    center = jnp.sum(row, axis=-1, keepdims=True) * (1.0 / D)
    centred = row - center
    spread_of = jnp.sum(centred * centred, axis=-1, keepdims=True) * (1.0 / D)
    rstd = lax.rsqrt(spread_of + 1e-05)
    return centred * rstd, rstd


def finish_rows(emb, cot, proj, grads, out, gin):
    row = emb[0].astype(F32)
    out[0] = (row + proj[...]).astype(BF16)
    unit, rstd = norm(row)
    grad = grads[...]
    mean = jnp.sum(grad, axis=-1, keepdims=True) * (1.0 / D)
    along = jnp.sum(grad * unit, axis=-1, keepdims=True) * (1.0 / D)
    gin[0] = (cot[0].astype(F32) + rstd * (grad - mean - unit * along)).astype(BF16)


def kernel(
    emb_in,
    cot_in,
    w_query,
    w_key,
    w_value,
    w_output,
    helpers,
    flag,
    live,
    proj_ref,
    grad_ref,
    emb,
    cot,
    proj,
    weights,
    normed,
    queries,
    keys,
    values,
    dattend,
    s_part,
    g_part,
    s_chain,
    g_chain,
    s_plane,
    g_plane,
    s_cross,
    g_cross,
    s_tot,
    g_tot,
    attend,
    probs,
    dlog,
    attended,
    dquery,
    dkey,
    dvalue,
    dnormed,
    send_sems,
    recv_sems,
    own_sems,
):
    g = lax.axis_index("grp")
    z = lax.axis_index("row")
    core = lax.rem(g, 2)
    x = lax.rem(lax.div(g, 2), 4)
    y = lax.div(g, 8)
    sib = g + 1 - 2 * core
    way_of_core = 1 - 2 * core
    plan = Plan()
    LAST_PLAN[:] = [plan]

    def at(group, row):
        return {"grp": group, "row": row}

    def chip(dx, dy):
        return at((rem(y + dy, 4) * 4 + rem(x + dx, 4)) * 2 + core, z)

    hops = {d: at(g, rem(z + d, ZN)) for d in Z_HOPS}
    around = {
        (dx, dy): chip(dx, dy) for dx in (1, -1, 0) for dy in (1, -1, 0) if dx != 0 or dy != 0
    }
    other = at(sib, z)
    x_step = 1 - 2 * lax.rem(x + core, 2)
    y_step = 1 - 2 * lax.rem(y + core, 2)
    partners = (
        (chip(x_step, 0), (("wx", 1, 1),)),
        (chip(0, y_step), (("wy", 1, 1),)),
        (chip(x_step, y_step), (("wx", 1, 1), ("wy", 1, 1))),
    )

    barrier = pltpu.get_barrier_semaphore()
    peers = [*hops.values(), *around.values(), other]
    for peer in peers:
        pl.semaphore_signal(barrier, inc=1, device_id=peer, device_id_type=MESH)

    started = [0]
    steps = [0]

    def send(ref, dst, peer, kb, path):
        index = started[0]
        copy = pltpu.make_async_remote_copy(
            src_ref=ref,
            dst_ref=dst,
            send_sem=send_sems.at[index],
            recv_sem=recv_sems.at[index],
            device_id=peer,
            device_id_type=MESH,
        )
        copy.start()
        started[0] += 1
        flight = Flight(copy, plan.book(kb, path))
        plan.out.append(flight)
        return flight

    own_rows = pl.ds(pl.multiple_of(z * SH, 16), SH)
    shards = [
        pltpu.make_async_copy(ref, weights.at[m, own_rows, :], own_sems.at[m])
        for m, ref in enumerate((w_query, w_key, w_value, w_output))
    ]
    get_emb = pltpu.make_async_copy(emb_in, emb, own_sems.at[4])
    get_cot = pltpu.make_async_copy(cot_in, cot, own_sems.at[5])
    for copy in (*shards, get_emb, get_cot):
        copy.start()
    for copy in shards:
        copy.wait()

    pl.semaphore_wait(barrier, len(peers))

    arrived = [0, 0]

    def weight_set(m, rank):
        def rows(k):
            return pl.ds(pl.multiple_of(rem(z - way_of_core * k, ZN) * SH, 16), SH)

        def piece(k):
            columns = pl.ds(pl.multiple_of(lax.rem(x, 2) * QC, 128), QC)
            return weights.at[2 * m + lax.rem(y, 2), rows(k), columns]

        def forward(k):
            for hop in W_TREE.get(k, ()):
                ref = piece(k)
                peer = at(g, rem(z + way_of_core * hop, ZN))
                path = (("up", hop, 1),)
                flight = send(ref, ref, peer, 36.9, path)
                plan.free["down"] = plan.free.get("down", 0.0) + hop * 0.369
                plan.spawn(rank, arrive(k + hop, flight))

        def arrive(k, flight):
            yield [flight]
            forward(k)
            ref = piece(k)
            yield [send(ref, ref, peer, 36.9, path) for peer, path in partners]
            if k < 8:
                ref = weights.at[pl.ds(2 * m, 2), rows(k), :]
                yield [send(ref, ref, other, 147.5, (("core", 1, 1),))]
            arrived[m] += 1

        forward(0)

    def chain_sum(part, chain, tree, p, blocks, counts, streams, rank, finished):
        kind = chain.dtype
        rows = chain.shape[3]
        edges = [0, rows] if streams == 1 else [0, PR, rows]
        left = [2 * streams]

        def term(lo, hi, chunk):
            pieces = []
            for i, block in enumerate(blocks):
                span = pl.ds(pl.multiple_of(block * HALF + chunk * PR, 16), PR)
                for half in range(2):
                    if lo <= (2 * i + half) * PR < hi:
                        pieces.append(part[half, span, :])
            if hi > 2 * len(blocks) * PR:
                pieces.append(counts)
            return jnp.concatenate(pieces, axis=0) if len(pieces) > 1 else pieces[0]

        nodes = (8, 7)
        below = [
            {
                k: [k + hop for hop in tree.get(k, ()) if k + hop <= nodes[way]]
                for k in range(nodes[way] + 1)
            }
            for way in range(2)
        ]

        def stream(way, lo, hi):
            span = pl.ds(lo, hi - lo)
            kb = (hi - lo) * L * (4 if kind == F32 else 2) / 1000.0
            sign = 1 - 2 * way
            above = {child: k for k, under in below[way].items() for child in under}
            flights = {}

            def pass_on(k):
                here = term(lo, hi, rem(z + sign * k, ZN))
                for child in below[way][k]:
                    here = here + chain[p, way, child - 1, span].astype(F32)
                slot = chain.at[p, way, 7 + k, span]
                slot[...] = here.astype(kind)
                plan.spend(0.04)
                hop = k - above[k]
                path = (("up" if way == 0 else "down", hop, 2),)
                landing = chain.at[p, way, k - 1, span]
                flights[k] = send(slot, landing, hops[sign * hop], kb, path)
                if all(child in flights for child in below[way][above[k]]):
                    plan.spawn(rank, node(above[k]))

            def node(k):
                yield [flights[child] for child in below[way][k]]
                if k > 0:
                    if kind == F32:
                        steps[0] += 1
                        lead()
                    pass_on(k)
                    return
                left[0] -= 1
                if left[0] == 0:
                    plan.spend(0.1)
                    total = term(0, rows, z)
                    for side in range(2):
                        for child in below[side][0]:
                            total = total + chain[p, side, child - 1].astype(F32)
                    finished(p, total)

            for k in range(nodes[way], 0, -1):
                if not below[way][k]:
                    pass_on(k)

        for lo, hi in zip(edges[:-1], edges[1:]):
            for way in range(2):
                stream(way, lo, hi)

    def spread(buf, tree, p, rank, finished):
        left = [15]

        def piece(d):
            start = pl.multiple_of(p * HALF + rem(z + d, ZN) * PR, 16)
            return buf.at[:, pl.ds(start, PR), :]

        def forward(d):
            for hop in tree.get(d, ()):
                ref = piece(d)
                path = (("up", hop, 2),) if hop > 0 else (("down", -hop, 2),)
                flight = send(ref, ref, hops[hop], PR * 0.512, path)
                plan.spawn(rank, arrive(d - hop, flight))

        def arrive(d, flight):
            yield [flight]
            forward(d)
            left[0] -= 1
            if left[0] == 0:
                finished(p)

        forward(0)

    target = helpers[g]
    sib_target = helpers[sib]
    top_half = lax.broadcasted_iota(jnp.int32, (8, L), 0) < 4

    def plane_sum(plane, cross, total, p, pairs, rank, finished):
        rows = 2 * PR * pairs + (8 if p == 0 and plane.dtype == F32 else 0)
        tallied = rows > 2 * PR * pairs
        kb = rows * L * (4 if plane.dtype == F32 else 2) / 1000.0
        passed = []
        left = [8]
        whole = pl.ds(0, rows)
        plane[p, y, x, whole] = total[p, whole].astype(plane.dtype)

        def path(dx, dy):
            steps = []
            if dx != 0:
                steps.append(("x+" if dx > 0 else "x-", 1, 2))
            if dy != 0:
                steps.append(("y+" if dy > 0 else "y-", 1, 2))
            return steps

        def item(dx, dy, *span):
            return plane.at[(p, rem(y + dy, 4), rem(x + dx, 4), *span)]

        passes = {
            (-1, 0): ((1, 0),),
            (-1, 1): ((1, 0), (0, -1)),
            (1, -1): ((-1, 0), (0, 1)),
            (0, -1): ((0, 1),),
            (1, 1): ((-1, -1),),
        }

        def arrive(dx, dy, flight):
            yield [flight]
            for step in passes.get((-dx, -dy), ()):
                ref = item(-dx, -dy, whole)
                passed.append(send(ref, ref, around[step], kb, path(*step)))
            left[0] -= 1
            if left[0] == 0:
                plan.spawn(rank, finish())
                if plane.dtype == F32:
                    state["sent"] += 1
                    release()

        def sums(me, its_target):
            def step(slot, carry):
                b, a = lax.div(slot, 4), lax.rem(slot, 4)
                group = slot * 2 + core
                w_home = jnp.where(helpers[group] == me, 1.0, 0.0)
                w_own = jnp.where(its_target == group, 1.0, 0.0)
                w_help = jnp.where(helpers[group] == its_target, 1.0, 0.0)
                share = plane.at[p, b, a]
                sums_of, tally = list(carry[: 2 * pairs]), carry[2 * pairs :]
                for i in range(0, 2 * pairs, 2):
                    first = share[i * PR : (i + 1) * PR, :].astype(F32)
                    second = share[(i + 1) * PR : (i + 2) * PR, :].astype(F32)
                    sums_of[i] = sums_of[i] + w_home * second
                    sums_of[i + 1] = sums_of[i + 1] + w_own * first + w_help * second
                if tallied:
                    count = share[2 * PR : rows, :]
                    tally = (
                        tally[0] + w_home * count,
                        tally[1] + w_own * count,
                        tally[2] + w_help * count,
                    )
                return (*sums_of, *tally)

            zero = jnp.zeros((PR, L), F32)
            none = jnp.zeros((8, L), F32)
            carry = (zero,) * (2 * pairs) + ((none,) * 3 if tallied else ())
            carry = lax.fori_loop(0, 16, step, carry)
            plan.spend(0.3 * pairs)
            sums_of, tally = carry[: 2 * pairs], carry[2 * pairs :]
            if tallied:
                first = jnp.broadcast_to(tally[0][4:5, :], (8, L))
                second = jnp.broadcast_to(tally[1][0:1, :] + tally[2][4:5, :], (8, L))
                return sums_of, jnp.where(top_half, first, second)
            return sums_of, None

        def finish():
            yield list(passed)
            sums_of, tally = sums(sib, sib_target)
            for i in range(2 * pairs):
                cross[p, 0, i * PR : (i + 1) * PR, :] = sums_of[i]
            if tallied:
                cross[p, 0, 2 * PR : rows, :] = tally
            swap = send(
                cross.at[p, 0, whole],
                cross.at[p, 1, whole],
                other,
                rows * 0.512,
                (("core", 1, 1),),
            )
            sums_of, tally = sums(g, target)
            yield [swap]
            for i in range(2 * pairs):
                span = slice(i * PR, (i + 1) * PR)
                here = sums_of[i] + cross[p, 1, span, :]
                total[p, span, :] = total[p, span, :] + here if i % 2 == 0 else here
            if tallied:
                own = jnp.where(top_half, total[p, 2 * PR : rows, :], 0.0)
                total[p, 2 * PR : rows, :] = own + tally + cross[p, 1, 2 * PR : rows, :]
            plan.spend(0.1)
            finished(p)

        for step, peer in around.items():
            own = item(0, 0, whole)
            plan.spawn(rank, arrive(*step, send(own, own, peer, kb, path(*step))))

    is_home = [(flag[r] == 0) | (target == g) for r in range(RDEV)]
    alive = [live[r].astype(F32) for r in range(RDEV)]
    home_f = [jnp.where(h, 1.0, 0.0) for h in is_home]
    help_f = [1.0 - h for h in home_f]
    home_live = [h * a for h, a in zip(home_f, alive)]
    help_live = [h * a for h, a in zip(help_f, alive)]
    home_count = home_live[0] + home_live[1] + home_live[2] + home_live[3]
    help_count = help_live[0] + help_live[1] + help_live[2] + help_live[3]
    counts = jnp.where(top_half, home_count, help_count)

    first_half = (lax.broadcasted_iota(jnp.int32, (1, L), 1) < L // 2).astype(F32)
    halves = (first_half, 1.0 - first_half)

    def normalise():
        plan.spend(1.2)

        @pl.loop(0, RDEV)
        def _(r):
            rows = pl.ds(pl.multiple_of(r * L, L), L)
            normed[rows, :] = norm(emb[r].astype(F32))[0].astype(BF16)

    def project(m, dst, p):
        plan.spend(0.5)

        @pl.loop(0, 2)
        def _(n):
            rows = pl.ds(pl.multiple_of(n * 256, 256), 256)
            cols = pl.ds(p * QC, QC)
            dst[rows, cols] = dot(normed[rows, :], weights[m, :, cols]).astype(BF16)

    def project_back():
        plan.spend(0.8)

        @pl.loop(0, 3)
        def _(n):
            cols = pl.ds(pl.multiple_of(n * 256, 256), 256)
            dattend[:, cols] = dot_t(cot[...].reshape(RDEV * L, D), weights[3, cols, :]).astype(
                BF16
            )

    def pair_terms(left, right, home_w, help_w, part, centre, first, last):
        plan.spend(0.1 * (last - first))
        masks = [
            [(half * w).astype(BF16) for w in ws] for ws in (home_w, help_w) for half in halves
        ]

        @pl.loop(first, last)
        def _(p):
            cols = pl.ds(pl.multiple_of(p * L, L), L)
            lefts = jnp.concatenate(
                [left[r * L : (r + 1) * L, cols] for r in range(RDEV)], axis=1
            )
            rights = [right[r * L : (r + 1) * L, cols] for r in range(RDEV)]
            for v in range(4):
                masked = jnp.concatenate(
                    [rights[r] * masks[v][r] for r in range(RDEV)], axis=1
                )
                rows = pl.ds(pl.multiple_of(p * 2 * L + (v % 2) * L, L), L)
                sums = dot_t(lefts, masked)
                if centre:
                    sums = sums - jnp.sum(sums, axis=-1, keepdims=True) * (1.0 / L)
                part[v // 2, rows, :] = sums

    def split_heads(ref, r, cols):
        piece = ref[r * L : (r + 1) * L, cols]
        return jnp.concatenate([piece * half.astype(BF16) for half in halves], axis=0)

    def apply_pair(mix, first, first_out, second, second_out, scale, p):
        cols = pl.ds(pl.multiple_of(p * L, L), L)
        tiles = [
            [mix[e, pl.ds(pl.multiple_of((2 * p + h) * L, L), L), :] for h in range(2)]
            for e in range(2)
        ]
        straight = [jnp.concatenate(t, axis=1) for t in tiles]
        turned = [jnp.concatenate([t.T for t in ts], axis=1) for ts in tiles]
        for r in range(RDEV):
            rows = slice(r * L, (r + 1) * L)
            pick = jnp.where(is_home[r], straight[0], straight[1])
            one = dot(pick, split_heads(first, r, cols))
            pick = jnp.where(is_home[r], turned[0], turned[1])
            two = dot(pick, split_heads(second, r, cols))
            if scale is not None:
                one, two = one * scale[r], two * scale[r]
            first_out[rows, cols] = one.astype(BF16)
            second_out[rows, cols] = two.astype(BF16)

    held = []
    state = {"sent": 0, "soft": set(), "grad": set(), "probs": 0, "dlog": 0, "applied": False}
    state.update(terms=False, led=False, late=list(range(PARTS)))
    scalings = []
    put_proj = pltpu.make_async_copy(proj, proj_ref, own_sems.at[6])

    def share_rows(p):
        return pl.ds(pl.multiple_of(p * HALF + z * PR, 16), PR)

    def scores_summed(p, total):
        s_tot[p, 0 : total.shape[0], :] = total
        plan.mark(("scores summed", p))
        plane_sum(s_plane, s_cross, s_tot, p, 1, 1, soften)

    def grads_summed(p, total):
        g_tot[p] = total
        plan.mark(("grads summed", p))
        held.append(p)
        release()

    def release():
        while held and state["sent"] >= HOLD:
            i = held.pop(0)
            plane_sum(g_plane, g_cross, g_tot, i, len(G_BLOCKS[i]), 2, grads_known)

    def soften(p):
        plan.spend(0.5 / PARTS)
        plan.mark(("softmax", p))
        for e in range(2):
            if p == 0:
                depth = s_tot[0, 2 * PR + 4 * e : 2 * PR + 4 * e + 1, :]
                scalings.append(1.0 / (8.0 * jnp.sqrt(depth)))
            logits = s_tot[p, e * PR : (e + 1) * PR, :] * scalings[e]
            top = jnp.exp(logits - jnp.max(logits, axis=-1, keepdims=True))
            share = top / jnp.sum(top, axis=-1, keepdims=True)
            attend[e, p * PR : (p + 1) * PR, :] = share
            probs[e, share_rows(p), :] = share.astype(BF16)
        state["soft"].add(p)
        spread(probs, Z_TREE, p, 3, probs_here)
        differentiate(p)

    def grads_known(i):
        for p in G_BLOCKS[i]:
            state["grad"].add(p)
            differentiate(p)

    def grads_of(p, e):
        for i, blocks in enumerate(G_BLOCKS):
            if p in blocks:
                start = (2 * blocks.index(p) + e) * PR
                return g_tot[i, start : start + PR, :]

    def differentiate(p):
        if p not in state["soft"] or p not in state["grad"]:
            return
        plan.spend(0.4 / PARTS)
        plan.mark(("dlogit", p))
        for e in range(2):
            share = attend[e, p * PR : (p + 1) * PR, :]
            grads = grads_of(p, e)
            mean = jnp.sum(grads * share, axis=-1, keepdims=True)
            dlog[e, share_rows(p), :] = (share * (grads - mean) * scalings[e]).astype(BF16)
        spread(dlog, Z_TREE, p, 2, dlog_here)

    def probs_here(p):
        plan.mark(("probs", p))
        plan.spawn(9, apply_probs(p))

    def dlog_here(p):
        state["dlog"] += 1
        plan.mark(("dlog", p))
        if state["dlog"] < PARTS:
            state["late"].remove(p)
            plan.spawn(8, apply_dlog(p))

    def in_chunks(p, work):
        for first in range(p * PP, p * PP + PP, CHUNK):
            plan.spend(0.5 * CHUNK)

            @pl.loop(first, first + CHUNK)
            def _(pair):
                work(pair)

            yield []

    def apply_dlog(p):
        yield []
        yield from in_chunks(
            p, lambda pair: apply_pair(dlog, keys, dquery, queries, dkey, alive, pair)
        )

    def apply_probs(p):
        yield []
        yield from in_chunks(
            p, lambda pair: apply_pair(probs, values, attended, dattend, dvalue, None, pair)
        )
        state["probs"] += 1
        if state["probs"] < PARTS:
            return
        plan.spend(0.8)

        @pl.loop(0, 3)
        def _(n):
            cols = pl.ds(pl.multiple_of(n * 256, 256), 256)
            proj[:, cols] = dot(attended[...], weights[3, :, cols])

        put_proj.start()
        yield []
        plan.spend(0.8)

        @pl.loop(0, 3)
        def _(n):
            cols = pl.ds(pl.multiple_of(n * 256, 256), 256)
            dnormed[:, cols] = dot_t(dvalue[...], weights[2, cols, :])

        state["applied"] = True

    def grad_terms():
        yield []
        get_cot.wait()
        for p in range(PARTS):
            project(2, values, p)
            yield []
        project_back()
        yield []
        for p in range(PARTS):
            pair_terms(
                dattend, values, home_f, help_f, g_part, True, p * PP, p * PP + PP
            )
            yield []
        state["terms"] = True
        lead()

    def lead():
        if state["terms"] and steps[0] >= S_LEAD and not state["led"]:
            state["led"] = True
            for i, blocks in enumerate(G_BLOCKS):
                chain_sum(
                    g_part, g_chain, G_TREE, i, blocks, None, G_STREAMS, 2, grads_summed
                )

    def put_grad(n):
        cols = pl.ds(pl.multiple_of(n * 256, 256), 256)
        return pltpu.make_async_copy(dnormed.at[:, cols], grad_ref.at[:, cols], own_sems.at[7 + n])

    plan.spend(3.0)
    weight_set(0, 0)
    weight_set(1, 4)
    get_emb.wait()
    normalise()
    plan.run(lambda: arrived[0] == 8)
    plan.mark("weights 0")
    for p in range(PARTS):
        project(0, queries, p)
        project(1, keys, p)
        pair_terms(queries, keys, home_live, help_live, s_part, False, p * PP, p * PP + PP)
        chain = s_chain.at[:, :, :, 0 : 2 * PR + (8 if p == 0 else 0)]
        chain_sum(s_part, chain, S_TREE, p, (p,), counts, S_STREAMS, 1, scores_summed)
    plan.run(lambda: arrived[1] == 8)
    plan.mark("weights 1")
    plan.spawn(9, grad_terms())
    plan.run(lambda: state["dlog"] == PARTS and not plan.tasks)
    plan.mark("all here")
    plan.spend(1.5 * len(state["late"]) + 1.6 + 1.5 + 1.0)

    for p in state["late"]:

        @pl.loop(p * PP, p * PP + PP)
        def _(pair):
            apply_pair(dlog, keys, dquery, queries, dkey, alive, pair)

    @pl.loop(0, 3)
    def _(n):
        cols = pl.ds(pl.multiple_of(n * 256, 256), 256)
        dnormed[:, cols] += dot_t(dquery[...], weights[0, cols, :]) + dot_t(
            dkey[...], weights[1, cols, :]
        )
        put_grad(n).start()

    for flight in plan.out:
        flight.copy.wait_send()
    put_proj.wait()
    for n in range(3):
        put_grad(n).wait()


def per_device(*args):
    rows = RDEV * L
    hbm = pl.BlockSpec(memory_space=pl.ANY)
    smem = pl.BlockSpec(memory_space=pltpu.SMEM)
    wide = jax.ShapeDtypeStruct((rows, D), F32)
    flat = pltpu.VMEM((rows, D), BF16)
    block = pltpu.VMEM((RDEV, L, D), BF16)
    s_rows, g_rows = 2 * PR + 8, 2 * PR * len(G_BLOCKS[0])
    scratch = [
        block,
        block,
        pltpu.VMEM((rows, D), F32),
        pltpu.VMEM((4, D, D), BF16),
        flat,
        flat,
        flat,
        flat,
        flat,
        pltpu.VMEM((2, HEADS * L, L), F32),
        pltpu.VMEM((2, HEADS * L, L), F32),
        pltpu.VMEM((PARTS, 2, 16, s_rows, L), F32),
        pltpu.VMEM((len(G_BLOCKS), 2, 16, g_rows, L), BF16),
        pltpu.VMEM((PARTS, 4, 4, s_rows, L), F32),
        pltpu.VMEM((len(G_BLOCKS), 4, 4, g_rows, L), BF16),
        pltpu.VMEM((PARTS, 2, s_rows, L), F32),
        pltpu.VMEM((len(G_BLOCKS), 2, g_rows, L), F32),
        pltpu.VMEM((PARTS, s_rows, L), F32),
        pltpu.VMEM((len(G_BLOCKS), g_rows, L), F32),
        pltpu.VMEM((2, CH, L), F32),
        pltpu.VMEM((2, HEADS * L, L), BF16),
        pltpu.VMEM((2, HEADS * L, L), BF16),
        flat,
        flat,
        flat,
        flat,
        pltpu.VMEM((rows, D), F32),
        pltpu.SemaphoreType.DMA((N_SEM,)),
        pltpu.SemaphoreType.DMA((N_SEM,)),
        pltpu.SemaphoreType.DMA((10,)),
    ]
    proj, grads = pl.pallas_call(
        kernel,
        out_shape=(wide, wide),
        in_specs=[hbm] * 6 + [smem] * 3,
        out_specs=(hbm, hbm),
        scratch_shapes=scratch,
        compiler_params=pltpu.CompilerParams(
            collective_id=0, has_side_effects=True, vmem_limit_bytes=60 * 1024 * 1024
        ),
    )(*args)
    shape = jax.ShapeDtypeStruct((RDEV, L, D), BF16)
    row = pl.BlockSpec((1, L, D), lambda r: (r, 0, 0))
    flat_row = pl.BlockSpec((L, D), lambda r: (r, 0))
    return pl.pallas_call(
        finish_rows,
        grid=(RDEV,),
        out_shape=(shape, shape),
        in_specs=[row, row, flat_row, flat_row],
        out_specs=(row, row),
        compiler_params=pltpu.CompilerParams(vmem_limit_bytes=60 * 1024 * 1024),
    )(args[0], args[1], proj, grads)


def solution(mesh):
    placed = (
        P(("grp", "row"), None, None),
        P(("grp", "row"), None, None),
        P("row", None),
        P("row", None),
        P("row", None),
        P("row", None),
        P(),
        P(("grp", "row")),
        P(("grp", "row")),
    )
    return jax.shard_map(
        per_device,
        mesh=mesh,
        in_specs=placed,
        out_specs=(P(("grp", "row"), None, None), P(("grp", "row"), None, None)),
        check_vma=False,
    )
```

```python
import functools

import jax
import jax.numpy as jnp
from jax import lax
from jax.experimental import pallas as pl
from jax.experimental.pallas import tpu as pltpu
from jax.sharding import PartitionSpec as P

HEADS = 12
RDEV = 4
L = 128
D = 768
ZN = 16
SH = D // ZN
QC = D // 2
CH = HEADS * L // ZN
PAIRS = HEADS // 2
MESH = pl.DeviceIdType.MESH
F32 = jnp.float32
BF16 = jnp.bfloat16
N_SEM = 400

PARTS = 2
PR = CH // PARTS
HALF = HEADS * L // PARTS
PP = PAIRS // PARTS
CHUNK = 3
S_STREAMS = 2
G_STREAMS = 1

W_TREE = {0: (3, 1, 2), 3: (3, 1, 2), 6: (1, 2)}
Z_TREE = {
    0: (3, -3, 1, -1),
    -3: (3, 1, -1),
    3: (-3, -1, 1),
    -6: (1, -1),
    6: (-1, 1),
    -7: (1,),
}
S_TREE = {0: (1, 2), **{k: (1,) for k in range(2, 8)}}
G_TREE = {k: (1,) for k in range(8)}
S_LEAD = 12
HOLD = 2
Z_HOPS = (1, -1, 2, -2, 3, -3)


START = 0.13
G_BLOCKS = ((0,), (1,))


class Plan:
    def __init__(self):
        self.now = 0.0
        self.free = {}
        self.tasks = []
        self.out = []
        self.marks = {}

    def book(self, kb, path):
        self.now += START
        start, hops = self.now, 0
        for link, units, cores in path:
            hops += units
            span = kb / 600.0 if link == "core" else units * kb * cores / 100.0
            start = max(start, self.free.get(link, 0.0)) + span
            self.free[link] = start
        return start + 2.5 + 0.15 * (hops - 1)

    def spend(self, time):
        self.now += time

    def mark(self, name):
        self.marks[name] = round(self.now, 1)

    def spawn(self, rank, task):
        wanted = next(task, None)
        if wanted is not None:
            self.tasks.append([rank, task, wanted])

    def run(self, done):
        while not done():
            best = None
            for entry in self.tasks:
                due = max([copy.due for copy in entry[2]], default=0.0)
                key = (max(due, self.now), entry[0], due)
                if best is None or key < best[0]:
                    best = (key, entry)
            key, entry = best
            while self.out and self.now + 0.1 < key[0] and self.out[0].due < self.now:
                self.out.pop(0).copy.wait_send()
                self.now += 0.03
            self.now = max(self.now, key[0]) + 0.05 * len(entry[2])
            for copy in entry[2]:
                copy.wait()
            wanted = next(entry[1], None)
            if wanted is None:
                self.tasks.remove(entry)
            else:
                entry[2] = wanted


LAST_PLAN = []


class Flight:
    def __init__(self, copy, due):
        self.copy, self.due = copy, due

    def wait(self):
        self.copy.wait_recv()


def rem(a, n):
    return lax.rem(a + n, n)


def dot(a, b):
    return lax.dot_general(a, b, (((1,), (0,)), ((), ())), preferred_element_type=F32)


def dot_t(a, b):
    return lax.dot_general(a, b, (((1,), (1,)), ((), ())), preferred_element_type=F32)


def norm(row):
    center = jnp.sum(row, axis=-1, keepdims=True) * (1.0 / D)
    centred = row - center
    spread_of = jnp.sum(centred * centred, axis=-1, keepdims=True) * (1.0 / D)
    rstd = lax.rsqrt(spread_of + 1e-05)
    return centred * rstd, rstd


def kernel(
    emb_in,
    cot_in,
    w_query,
    w_key,
    w_value,
    w_output,
    helpers,
    flag,
    live,
    proj_ref,
    gin_ref,
    emb,
    cot,
    proj,
    gin,
    unit,
    scale_in,
    weights,
    normed,
    queries,
    keys,
    values,
    dattend,
    s_part,
    g_part,
    s_chain,
    g_chain,
    s_plane,
    g_plane,
    s_cross,
    g_cross,
    s_tot,
    g_tot,
    attend,
    probs,
    dlog,
    attended,
    dquery,
    dkey,
    dvalue,
    dnormed,
    send_sems,
    recv_sems,
    own_sems,
):
    g = lax.axis_index("grp")
    z = lax.axis_index("row")
    core = lax.rem(g, 2)
    x = lax.rem(lax.div(g, 2), 4)
    y = lax.div(g, 8)
    sib = g + 1 - 2 * core
    way_of_core = 1 - 2 * core
    plan = Plan()
    LAST_PLAN[:] = [plan]

    def at(group, row):
        return {"grp": group, "row": row}

    def chip(dx, dy):
        return at((rem(y + dy, 4) * 4 + rem(x + dx, 4)) * 2 + core, z)

    hops = {d: at(g, rem(z + d, ZN)) for d in Z_HOPS}
    around = {
        (dx, dy): chip(dx, dy) for dx in (1, -1, 0) for dy in (1, -1, 0) if dx != 0 or dy != 0
    }
    other = at(sib, z)
    x_step = 1 - 2 * lax.rem(x + core, 2)
    y_step = 1 - 2 * lax.rem(y + core, 2)
    partners = (
        (chip(x_step, 0), (("wx", 1, 1),)),
        (chip(0, y_step), (("wy", 1, 1),)),
        (chip(x_step, y_step), (("wx", 1, 1), ("wy", 1, 1))),
    )

    barrier = pltpu.get_barrier_semaphore()
    peers = [*hops.values(), *around.values(), other]
    for peer in peers:
        pl.semaphore_signal(barrier, inc=1, device_id=peer, device_id_type=MESH)

    started = [0]
    steps = [0]

    def send(ref, dst, peer, kb, path):
        index = started[0]
        copy = pltpu.make_async_remote_copy(
            src_ref=ref,
            dst_ref=dst,
            send_sem=send_sems.at[index],
            recv_sem=recv_sems.at[index],
            device_id=peer,
            device_id_type=MESH,
        )
        copy.start()
        started[0] += 1
        flight = Flight(copy, plan.book(kb, path))
        plan.out.append(flight)
        return flight

    own_rows = pl.ds(pl.multiple_of(z * SH, 16), SH)
    shards = [
        pltpu.make_async_copy(ref, weights.at[m, own_rows, :], own_sems.at[m])
        for m, ref in enumerate((w_query, w_key, w_value, w_output))
    ]
    get_emb = pltpu.make_async_copy(emb_in, emb, own_sems.at[4])
    get_cot = pltpu.make_async_copy(cot_in, cot, own_sems.at[5])
    for copy in (*shards, get_emb, get_cot):
        copy.start()
    for copy in shards:
        copy.wait()

    pl.semaphore_wait(barrier, len(peers))

    arrived = [0, 0]

    def weight_set(m, rank):
        def rows(k):
            return pl.ds(pl.multiple_of(rem(z - way_of_core * k, ZN) * SH, 16), SH)

        def piece(k):
            columns = pl.ds(pl.multiple_of(lax.rem(x, 2) * QC, 128), QC)
            return weights.at[2 * m + lax.rem(y, 2), rows(k), columns]

        def forward(k):
            for hop in W_TREE.get(k, ()):
                ref = piece(k)
                peer = at(g, rem(z + way_of_core * hop, ZN))
                path = (("up", hop, 1),)
                flight = send(ref, ref, peer, 36.9, path)
                plan.free["down"] = plan.free.get("down", 0.0) + hop * 0.369
                plan.spawn(rank, arrive(k + hop, flight))

        def arrive(k, flight):
            yield [flight]
            forward(k)
            ref = piece(k)
            yield [send(ref, ref, peer, 36.9, path) for peer, path in partners]
            if k < 8:
                ref = weights.at[pl.ds(2 * m, 2), rows(k), :]
                yield [send(ref, ref, other, 147.5, (("core", 1, 1),))]
            arrived[m] += 1

        forward(0)

    def chain_sum(part, chain, tree, p, blocks, counts, streams, rank, finished):
        kind = chain.dtype
        rows = chain.shape[3]
        edges = [0, rows] if streams == 1 else [0, PR, rows]
        left = [2 * streams]

        def term(lo, hi, chunk):
            pieces = []
            for i, block in enumerate(blocks):
                span = pl.ds(pl.multiple_of(block * HALF + chunk * PR, 16), PR)
                for half in range(2):
                    if lo <= (2 * i + half) * PR < hi:
                        pieces.append(part[half, span, :])
            if hi > 2 * len(blocks) * PR:
                pieces.append(counts)
            return jnp.concatenate(pieces, axis=0) if len(pieces) > 1 else pieces[0]

        nodes = (8, 7)
        below = [
            {
                k: [k + hop for hop in tree.get(k, ()) if k + hop <= nodes[way]]
                for k in range(nodes[way] + 1)
            }
            for way in range(2)
        ]

        def stream(way, lo, hi):
            span = pl.ds(lo, hi - lo)
            kb = (hi - lo) * L * (4 if kind == F32 else 2) / 1000.0
            sign = 1 - 2 * way
            above = {child: k for k, under in below[way].items() for child in under}
            flights = {}

            def pass_on(k):
                here = term(lo, hi, rem(z + sign * k, ZN))
                for child in below[way][k]:
                    here = here + chain[p, way, child - 1, span].astype(F32)
                slot = chain.at[p, way, 7 + k, span]
                slot[...] = here.astype(kind)
                plan.spend(0.04)
                hop = k - above[k]
                path = (("up" if way == 0 else "down", hop, 2),)
                landing = chain.at[p, way, k - 1, span]
                flights[k] = send(slot, landing, hops[sign * hop], kb, path)
                if all(child in flights for child in below[way][above[k]]):
                    plan.spawn(rank, node(above[k]))

            def node(k):
                yield [flights[child] for child in below[way][k]]
                if k > 0:
                    if kind == F32:
                        steps[0] += 1
                        lead()
                    pass_on(k)
                    return
                left[0] -= 1
                if left[0] == 0:
                    plan.spend(0.1)
                    total = term(0, rows, z)
                    for side in range(2):
                        for child in below[side][0]:
                            total = total + chain[p, side, child - 1].astype(F32)
                    finished(p, total)

            for k in range(nodes[way], 0, -1):
                if not below[way][k]:
                    pass_on(k)

        for lo, hi in zip(edges[:-1], edges[1:]):
            for way in range(2):
                stream(way, lo, hi)

    def spread(buf, tree, p, rank, finished):
        left = [15]

        def piece(d):
            start = pl.multiple_of(p * HALF + rem(z + d, ZN) * PR, 16)
            return buf.at[:, pl.ds(start, PR), :]

        def forward(d):
            for hop in tree.get(d, ()):
                ref = piece(d)
                path = (("up", hop, 2),) if hop > 0 else (("down", -hop, 2),)
                flight = send(ref, ref, hops[hop], PR * 0.512, path)
                plan.spawn(rank, arrive(d - hop, flight))

        def arrive(d, flight):
            yield [flight]
            forward(d)
            left[0] -= 1
            if left[0] == 0:
                finished(p)

        forward(0)

    target = helpers[g]
    sib_target = helpers[sib]
    top_half = lax.broadcasted_iota(jnp.int32, (8, L), 0) < 4

    def plane_sum(plane, cross, total, p, pairs, rank, finished):
        rows = 2 * PR * pairs + (8 if p == 0 and plane.dtype == F32 else 0)
        tallied = rows > 2 * PR * pairs
        kb = rows * L * (4 if plane.dtype == F32 else 2) / 1000.0
        passed = []
        left = [8]
        whole = pl.ds(0, rows)
        plane[p, y, x, whole] = total[p, whole].astype(plane.dtype)

        def path(dx, dy):
            steps = []
            if dx != 0:
                steps.append(("x+" if dx > 0 else "x-", 1, 2))
            if dy != 0:
                steps.append(("y+" if dy > 0 else "y-", 1, 2))
            return steps

        def item(dx, dy, *span):
            return plane.at[(p, rem(y + dy, 4), rem(x + dx, 4), *span)]

        passes = {
            (-1, 0): ((1, 0),),
            (-1, 1): ((1, 0), (0, -1)),
            (1, -1): ((-1, 0), (0, 1)),
            (0, -1): ((0, 1),),
            (1, 1): ((-1, -1),),
        }

        def arrive(dx, dy, flight):
            yield [flight]
            for step in passes.get((-dx, -dy), ()):
                ref = item(-dx, -dy, whole)
                passed.append(send(ref, ref, around[step], kb, path(*step)))
            left[0] -= 1
            if left[0] == 0:
                plan.spawn(rank, finish())
                if plane.dtype == F32:
                    state["sent"] += 1
                    release()

        def sums(me, its_target):
            def step(slot, carry):
                b, a = lax.div(slot, 4), lax.rem(slot, 4)
                group = slot * 2 + core
                w_home = jnp.where(helpers[group] == me, 1.0, 0.0)
                w_own = jnp.where(its_target == group, 1.0, 0.0)
                w_help = jnp.where(helpers[group] == its_target, 1.0, 0.0)
                share = plane.at[p, b, a]
                sums_of, tally = list(carry[: 2 * pairs]), carry[2 * pairs :]
                for i in range(0, 2 * pairs, 2):
                    first = share[i * PR : (i + 1) * PR, :].astype(F32)
                    second = share[(i + 1) * PR : (i + 2) * PR, :].astype(F32)
                    sums_of[i] = sums_of[i] + w_home * second
                    sums_of[i + 1] = sums_of[i + 1] + w_own * first + w_help * second
                if tallied:
                    count = share[2 * PR : rows, :]
                    tally = (
                        tally[0] + w_home * count,
                        tally[1] + w_own * count,
                        tally[2] + w_help * count,
                    )
                return (*sums_of, *tally)

            zero = jnp.zeros((PR, L), F32)
            none = jnp.zeros((8, L), F32)
            carry = (zero,) * (2 * pairs) + ((none,) * 3 if tallied else ())
            carry = lax.fori_loop(0, 16, step, carry)
            plan.spend(0.3 * pairs)
            sums_of, tally = carry[: 2 * pairs], carry[2 * pairs :]
            if tallied:
                first = jnp.broadcast_to(tally[0][4:5, :], (8, L))
                second = jnp.broadcast_to(tally[1][0:1, :] + tally[2][4:5, :], (8, L))
                return sums_of, jnp.where(top_half, first, second)
            return sums_of, None

        def finish():
            yield list(passed)
            sums_of, tally = sums(sib, sib_target)
            for i in range(2 * pairs):
                cross[p, 0, i * PR : (i + 1) * PR, :] = sums_of[i]
            if tallied:
                cross[p, 0, 2 * PR : rows, :] = tally
            swap = send(
                cross.at[p, 0, whole],
                cross.at[p, 1, whole],
                other,
                rows * 0.512,
                (("core", 1, 1),),
            )
            sums_of, tally = sums(g, target)
            yield [swap]
            for i in range(2 * pairs):
                span = slice(i * PR, (i + 1) * PR)
                here = sums_of[i] + cross[p, 1, span, :]
                total[p, span, :] = total[p, span, :] + here if i % 2 == 0 else here
            if tallied:
                own = jnp.where(top_half, total[p, 2 * PR : rows, :], 0.0)
                total[p, 2 * PR : rows, :] = own + tally + cross[p, 1, 2 * PR : rows, :]
            plan.spend(0.1)
            finished(p)

        for step, peer in around.items():
            own = item(0, 0, whole)
            plan.spawn(rank, arrive(*step, send(own, own, peer, kb, path(*step))))

    is_home = [(flag[r] == 0) | (target == g) for r in range(RDEV)]
    alive = [live[r].astype(F32) for r in range(RDEV)]
    home_f = [jnp.where(h, 1.0, 0.0) for h in is_home]
    help_f = [1.0 - h for h in home_f]
    home_live = [h * a for h, a in zip(home_f, alive)]
    help_live = [h * a for h, a in zip(help_f, alive)]
    home_count = home_live[0] + home_live[1] + home_live[2] + home_live[3]
    help_count = help_live[0] + help_live[1] + help_live[2] + help_live[3]
    counts = jnp.where(top_half, home_count, help_count)

    first_half = (lax.broadcasted_iota(jnp.int32, (1, L), 1) < L // 2).astype(F32)
    halves = (first_half, 1.0 - first_half)

    def normalise():
        plan.spend(1.2)

        @pl.loop(0, RDEV)
        def _(r):
            rows = pl.ds(pl.multiple_of(r * L, L), L)
            here, rstd = norm(emb[r].astype(F32))
            unit[rows, :] = here
            scale_in[rows, :] = jnp.broadcast_to(rstd, (L, L))
            normed[rows, :] = here.astype(BF16)

    def project(m, dst, p):
        plan.spend(0.5)

        @pl.loop(0, 2)
        def _(n):
            rows = pl.ds(pl.multiple_of(n * 256, 256), 256)
            cols = pl.ds(p * QC, QC)
            dst[rows, cols] = dot(normed[rows, :], weights[m, :, cols]).astype(BF16)

    def project_back():
        plan.spend(0.8)

        @pl.loop(0, 3)
        def _(n):
            cols = pl.ds(pl.multiple_of(n * 256, 256), 256)
            dattend[:, cols] = dot_t(cot[...].reshape(RDEV * L, D), weights[3, cols, :]).astype(
                BF16
            )

    def pair_terms(left, right, home_w, help_w, part, centre, first, last):
        plan.spend(0.1 * (last - first))
        masks = [
            [(half * w).astype(BF16) for w in ws] for ws in (home_w, help_w) for half in halves
        ]

        @pl.loop(first, last)
        def _(p):
            cols = pl.ds(pl.multiple_of(p * L, L), L)
            lefts = jnp.concatenate(
                [left[r * L : (r + 1) * L, cols] for r in range(RDEV)], axis=1
            )
            rights = [right[r * L : (r + 1) * L, cols] for r in range(RDEV)]
            for v in range(4):
                masked = jnp.concatenate(
                    [rights[r] * masks[v][r] for r in range(RDEV)], axis=1
                )
                rows = pl.ds(pl.multiple_of(p * 2 * L + (v % 2) * L, L), L)
                sums = dot_t(lefts, masked)
                if centre:
                    sums = sums - jnp.sum(sums, axis=-1, keepdims=True) * (1.0 / L)
                part[v // 2, rows, :] = sums

    def split_heads(ref, r, cols):
        piece = ref[r * L : (r + 1) * L, cols]
        return jnp.concatenate([piece * half.astype(BF16) for half in halves], axis=0)

    def apply_pair(mix, first, first_out, second, second_out, scale, p):
        cols = pl.ds(pl.multiple_of(p * L, L), L)
        tiles = [
            [mix[e, pl.ds(pl.multiple_of((2 * p + h) * L, L), L), :] for h in range(2)]
            for e in range(2)
        ]
        straight = [jnp.concatenate(t, axis=1) for t in tiles]
        turned = [jnp.concatenate([t.T for t in ts], axis=1) for ts in tiles]
        for r in range(RDEV):
            rows = slice(r * L, (r + 1) * L)
            pick = jnp.where(is_home[r], straight[0], straight[1])
            one = dot(pick, split_heads(first, r, cols))
            pick = jnp.where(is_home[r], turned[0], turned[1])
            two = dot(pick, split_heads(second, r, cols))
            if scale is not None:
                one, two = one * scale[r], two * scale[r]
            first_out[rows, cols] = one.astype(BF16)
            second_out[rows, cols] = two.astype(BF16)

    held = []
    state = {"sent": 0, "soft": set(), "grad": set(), "probs": 0, "dlog": 0, "applied": False}
    state.update(terms=False, led=False, late=list(range(PARTS)))
    scalings = []
    put_proj = pltpu.make_async_copy(proj, proj_ref, own_sems.at[6])

    def share_rows(p):
        return pl.ds(pl.multiple_of(p * HALF + z * PR, 16), PR)

    def scores_summed(p, total):
        s_tot[p, 0 : total.shape[0], :] = total
        plan.mark(("scores summed", p))
        plane_sum(s_plane, s_cross, s_tot, p, 1, 1, soften)

    def grads_summed(p, total):
        g_tot[p] = total
        plan.mark(("grads summed", p))
        held.append(p)
        release()

    def release():
        while held and state["sent"] >= HOLD:
            i = held.pop(0)
            plane_sum(g_plane, g_cross, g_tot, i, len(G_BLOCKS[i]), 2, grads_known)

    def soften(p):
        plan.spend(0.5 / PARTS)
        plan.mark(("softmax", p))
        for e in range(2):
            if p == 0:
                depth = s_tot[0, 2 * PR + 4 * e : 2 * PR + 4 * e + 1, :]
                scalings.append(1.0 / (8.0 * jnp.sqrt(depth)))
            logits = s_tot[p, e * PR : (e + 1) * PR, :] * scalings[e]
            top = jnp.exp(logits - jnp.max(logits, axis=-1, keepdims=True))
            share = top / jnp.sum(top, axis=-1, keepdims=True)
            attend[e, p * PR : (p + 1) * PR, :] = share
            probs[e, share_rows(p), :] = share.astype(BF16)
        state["soft"].add(p)
        spread(probs, Z_TREE, p, 3, probs_here)
        differentiate(p)

    def grads_known(i):
        for p in G_BLOCKS[i]:
            state["grad"].add(p)
            differentiate(p)

    def grads_of(p, e):
        for i, blocks in enumerate(G_BLOCKS):
            if p in blocks:
                start = (2 * blocks.index(p) + e) * PR
                return g_tot[i, start : start + PR, :]

    def differentiate(p):
        if p not in state["soft"] or p not in state["grad"]:
            return
        plan.spend(0.4 / PARTS)
        plan.mark(("dlogit", p))
        for e in range(2):
            share = attend[e, p * PR : (p + 1) * PR, :]
            grads = grads_of(p, e)
            mean = jnp.sum(grads * share, axis=-1, keepdims=True)
            dlog[e, share_rows(p), :] = (share * (grads - mean) * scalings[e]).astype(BF16)
        spread(dlog, Z_TREE, p, 2, dlog_here)

    def probs_here(p):
        plan.mark(("probs", p))
        plan.spawn(9, apply_probs(p))

    def dlog_here(p):
        state["dlog"] += 1
        plan.mark(("dlog", p))
        if state["dlog"] < PARTS:
            state["late"].remove(p)
            plan.spawn(8, apply_dlog(p))

    def in_chunks(p, work):
        for first in range(p * PP, p * PP + PP, CHUNK):
            plan.spend(0.5 * CHUNK)

            @pl.loop(first, first + CHUNK)
            def _(pair):
                work(pair)

            yield []

    def apply_dlog(p):
        yield []
        yield from in_chunks(
            p, lambda pair: apply_pair(dlog, keys, dquery, queries, dkey, alive, pair)
        )

    def apply_probs(p):
        yield []
        yield from in_chunks(
            p, lambda pair: apply_pair(probs, values, attended, dattend, dvalue, None, pair)
        )
        state["probs"] += 1
        if state["probs"] < PARTS:
            return
        plan.spend(0.8)

        @pl.loop(0, 3)
        def _(n):
            cols = pl.ds(pl.multiple_of(n * 256, 256), 256)
            proj[:, cols] = dot(attended[...], weights[3, :, cols])

        put_proj.start()
        yield []
        plan.spend(0.8)

        @pl.loop(0, 3)
        def _(n):
            cols = pl.ds(pl.multiple_of(n * 256, 256), 256)
            dnormed[:, cols] = dot_t(dvalue[...], weights[2, cols, :])

        state["applied"] = True

    def grad_terms():
        yield []
        get_cot.wait()
        for p in range(PARTS):
            project(2, values, p)
            yield []
        project_back()
        yield []
        for p in range(PARTS):
            pair_terms(
                dattend, values, home_f, help_f, g_part, True, p * PP, p * PP + PP
            )
            yield []
        state["terms"] = True
        lead()

    def lead():
        if state["terms"] and steps[0] >= S_LEAD and not state["led"]:
            state["led"] = True
            for i, blocks in enumerate(G_BLOCKS):
                chain_sum(
                    g_part, g_chain, G_TREE, i, blocks, None, G_STREAMS, 2, grads_summed
                )

    plan.spend(3.0)
    weight_set(0, 0)
    weight_set(1, 4)
    get_emb.wait()
    normalise()
    plan.run(lambda: arrived[0] == 8)
    plan.mark("weights 0")
    for p in range(PARTS):
        project(0, queries, p)
        project(1, keys, p)
        pair_terms(queries, keys, home_live, help_live, s_part, False, p * PP, p * PP + PP)
        chain = s_chain.at[:, :, :, 0 : 2 * PR + (8 if p == 0 else 0)]
        chain_sum(s_part, chain, S_TREE, p, (p,), counts, S_STREAMS, 1, scores_summed)
    plan.run(lambda: arrived[1] == 8)
    plan.mark("weights 1")
    plan.spawn(9, grad_terms())
    plan.run(lambda: state["dlog"] == PARTS and not plan.tasks)
    plan.mark("all here")
    plan.spend(1.5 * len(state["late"]) + 1.6 + 1.5 + 1.0)

    for p in state["late"]:

        @pl.loop(p * PP, p * PP + PP)
        def _(pair):
            apply_pair(dlog, keys, dquery, queries, dkey, alive, pair)

    @pl.loop(0, 3)
    def _(n):
        cols = pl.ds(pl.multiple_of(n * 256, 256), 256)
        dnormed[:, cols] += dot_t(dquery[...], weights[0, cols, :]) + dot_t(
            dkey[...], weights[1, cols, :]
        )

    @pl.loop(0, RDEV)
    def _(r):
        rows = pl.ds(pl.multiple_of(r * L, L), L)
        grad, here = dnormed[rows, :], unit[rows, :]
        mean = jnp.sum(grad, axis=-1, keepdims=True) * (1.0 / D)
        along = jnp.sum(grad * here, axis=-1, keepdims=True) * (1.0 / D)
        back = scale_in[rows, 0:1] * (grad - mean - here * along)
        gin[r] = (cot[r].astype(F32) + back).astype(BF16)
        pltpu.make_async_copy(gin.at[r], gin_ref.at[r], own_sems.at[7 + r]).start()

    for flight in plan.out:
        flight.copy.wait_send()
    put_proj.wait()
    for r in range(RDEV):
        pltpu.make_async_copy(gin.at[r], gin_ref.at[r], own_sems.at[7 + r]).wait()


def per_device(*args):
    rows = RDEV * L
    hbm = pl.BlockSpec(memory_space=pl.ANY)
    smem = pl.BlockSpec(memory_space=pltpu.SMEM)
    wide = jax.ShapeDtypeStruct((rows, D), F32)
    shape = jax.ShapeDtypeStruct((RDEV, L, D), BF16)
    flat = pltpu.VMEM((rows, D), BF16)
    block = pltpu.VMEM((RDEV, L, D), BF16)
    s_rows, g_rows = 2 * PR + 8, 2 * PR * len(G_BLOCKS[0])
    scratch = [
        block,
        block,
        pltpu.VMEM((rows, D), F32),
        block,
        pltpu.VMEM((rows, D), F32),
        pltpu.VMEM((rows, L), F32),
        pltpu.VMEM((4, D, D), BF16),
        flat,
        flat,
        flat,
        flat,
        flat,
        pltpu.VMEM((2, HEADS * L, L), F32),
        pltpu.VMEM((2, HEADS * L, L), F32),
        pltpu.VMEM((PARTS, 2, 16, s_rows, L), F32),
        pltpu.VMEM((len(G_BLOCKS), 2, 16, g_rows, L), BF16),
        pltpu.VMEM((PARTS, 4, 4, s_rows, L), F32),
        pltpu.VMEM((len(G_BLOCKS), 4, 4, g_rows, L), BF16),
        pltpu.VMEM((PARTS, 2, s_rows, L), F32),
        pltpu.VMEM((len(G_BLOCKS), 2, g_rows, L), F32),
        pltpu.VMEM((PARTS, s_rows, L), F32),
        pltpu.VMEM((len(G_BLOCKS), g_rows, L), F32),
        pltpu.VMEM((2, CH, L), F32),
        pltpu.VMEM((2, HEADS * L, L), BF16),
        pltpu.VMEM((2, HEADS * L, L), BF16),
        flat,
        flat,
        flat,
        flat,
        pltpu.VMEM((rows, D), F32),
        pltpu.SemaphoreType.DMA((N_SEM,)),
        pltpu.SemaphoreType.DMA((N_SEM,)),
        pltpu.SemaphoreType.DMA((11,)),
    ]
    proj, gin = pl.pallas_call(
        kernel,
        out_shape=(wide, shape),
        in_specs=[hbm] * 6 + [smem] * 3,
        out_specs=(hbm, hbm),
        scratch_shapes=scratch,
        compiler_params=pltpu.CompilerParams(
            collective_id=0, has_side_effects=True, vmem_limit_bytes=60 * 1024 * 1024
        ),
    )(*args)
    out = (args[0].astype(F32) + proj.reshape(RDEV, L, D)).astype(BF16)
    return out, gin


def solution(mesh):
    placed = (
        P(("grp", "row"), None, None),
        P(("grp", "row"), None, None),
        P("row", None),
        P("row", None),
        P("row", None),
        P("row", None),
        P(),
        P(("grp", "row")),
        P(("grp", "row")),
    )
    return jax.shard_map(
        per_device,
        mesh=mesh,
        in_specs=placed,
        out_specs=(P(("grp", "row"), None, None), P(("grp", "row"), None, None)),
        check_vma=False,
    )
```
